32 devices in a mesh: seq: 2 (over x), ctx: 8 (over z, y), wsh: 2 (over core).
Axes of the slice: x: 2, y: 2, z: 4, core: 2. Of those that a mesh axis runs over, the one named last changes fastest.
Arguments:
- hidden_in: bfloat16 [2048, 4, 1024], P('ctx', ('seq', 'wsh')), may hold values from -6 to 6
- cotangent: bfloat16 [2048, 4, 1024], P('ctx', ('seq', 'wsh')), may hold values from -6 to 6
- query_key_value_weight: bfloat16 [1024, 2048], P('wsh'), may hold values from -0.1875 to 0.1875
- w_o: bfloat16 [1024, 1024], P('wsh'), may hold values from -3 to 3
- w_gu: bfloat16 [1024, 9216], P('wsh'), may hold values from -0.1875 to 0.1875
- w_down: bfloat16 [4608, 1024], P('wsh'), may hold values from -0.09375 to 0.09375
- g_attn: bfloat16 [1024], replicated, may hold values from 0.5 to 1.5
- g_ffn: bfloat16 [1024], replicated, may hold values from 0.5 to 1.5
- g_q: bfloat16 [64], replicated, may hold values from 0.5 to 1.5
- key_norm_gain: bfloat16 [64], replicated, may hold values from 0.5 to 1.5
- a_qkv: bfloat16 [8, 1024, 48], replicated, may hold values from -0.1875 to 0.1875
- b_q: bfloat16 [8, 16, 1024], replicated, may hold values from -0.75 to 0.75
- key_up_weight: bfloat16 [8, 16, 512], replicated, may hold values from -0.75 to 0.75
- value_up_weight: bfloat16 [8, 16, 512], replicated, may hold values from -0.75 to 0.75
- a_o: bfloat16 [8, 1024, 16], replicated, may hold values from -0.1875 to 0.1875
- b_o: bfloat16 [8, 16, 1024], replicated, may hold values from -6 to 6
- a_gu: bfloat16 [8, 1024, 32], replicated, may hold values from -0.1875 to 0.1875
- b_gu: bfloat16 [8, 2, 16, 4608], replicated, may hold values from -0.75 to 0.75
- a_down: bfloat16 [8, 4608, 16], replicated, may hold values from -0.09375 to 0.09375
- b_down: bfloat16 [8, 16, 1024], replicated, may hold values from -0.75 to 0.75
- set_index: int32 [4], replicated, may hold values from 0 to 7
- stretch_order: int32 [4, 16], P(('seq', 'wsh')), may hold values from 0 to 15, as said below
Outputs:
- layer_out: float32 [2048, 4, 1024], P('ctx', ('seq', 'wsh'))
- input_grad: float32 [2048, 4, 1024], P('ctx', ('seq', 'wsh'))
- grad_a_qkv: float32 [8, 1024, 48], replicated
- grad_b_q: float32 [8, 16, 1024], replicated
- grad_b_k: float32 [8, 16, 512], replicated
- grad_b_v: float32 [8, 16, 512], replicated
- grad_a_o: float32 [8, 1024, 16], replicated
- grad_b_o: float32 [8, 16, 1024], replicated
- grad_a_gu: float32 [8, 1024, 32], replicated
- grad_b_gu: float32 [8, 2, 16, 4608], replicated
- grad_a_down: float32 [8, 4608, 16], replicated
- grad_b_down: float32 [8, 16, 1024], replicated
The draws below stay inside these ranges and needn't reach their ends.
Inputs may be any that keep to these rules, and one draw needn't show every extreme that they name: `stretch_order`: in each row, slots 2 j and 2 j + 1 hold stretches c and 15 - c, where c over j = 0 to 7 is a permutation of 0 to 7 drawn for each sequence.
All inputs are finite; a program needn't handle non-finite values.
Results may differ from the reference program's by a relative error of at most 0.023.
Values may be sent and summed in bfloat16 or wider, within the bound.
No kernel may reach another device: no remote copies, remote signals or barrier semaphores. Data moves between devices by JAX's collectives and lax.ppermute only.
A program may use at most 384 MiB of HBM per device.

```python
import math
import jax
import jax.numpy as jnp
from jax import lax

MODEL_DIMENSION = 1024
QUERY_HEADS = 16
KEY_VALUE_HEADS = 8
HEAD_SIZE = 64
FF = 4608
ADAPTER_RANK = 16
ADAPTER_SETS = 8
CH = 128
LENGTH = 2048
NSEQ = 4
N_CTX = 8


def draw_stretch_order(key, part):
    seq_keys = jax.random.split(jax.random.fold_in(key, 17), NSEQ)

    def one_row(row_key):
        labels = jax.random.permutation(row_key, N_CTX).astype(jnp.int32)
        mirror = (2 * N_CTX - 1 - labels).astype(jnp.int32)
        return jnp.stack([labels, mirror], axis=1).reshape(2 * N_CTX)
    return jax.vmap(one_row)(seq_keys).astype(jnp.int32)


def with_ends(array, own_key, low, largest):
    longest = array.shape.index(max(array.shape))
    spots = []
    for shift in (0, 1):
        where = [jax.random.randint(jax.random.fold_in(own_key, axis), (), 0, length) for axis, length in enumerate(array.shape)]
        where[longest] = (where[longest] + shift) % array.shape[longest]
        spots.append(tuple(where))
    return array.at[spots[0]].set(low).at[spots[1]].set(largest)


def level_of(rng, dims, shards, smallest, high):
    def one(dim, parts):
        steps = jax.random.uniform(jax.random.fold_in(jax.random.fold_in(rng, 6), dim), (parts,), jnp.float32, smallest / len(shards), high / len(shards))
        return jnp.repeat(jnp.exp(steps), dims[dim] // parts).reshape((-1,) + (1,) * (len(dims) - dim - 1))

    level = one(*shards[0])
    for cut in shards[1:]:
        level = level * one(*cut)
    return level


def normal_values(stream_key, extent, spread, bound, pieces=(), held_as=jnp.bfloat16):
    factor_of = level_of(stream_key, extent, pieces, -0.22, 0.18) if pieces else 1.0
    values = jax.random.normal(stream_key, extent, jnp.float32) * spread * factor_of
    return jnp.minimum(jnp.maximum(values, -bound), bound).astype(held_as)


def setup_inputs(seed: int = 0) -> dict:
    keys = jax.random.split(jax.random.key(seed), 23)
    hidden_in = normal_values(keys[0], (LENGTH, NSEQ, MODEL_DIMENSION), 1.0, 6.0, ((0, 8), (1, 4)))
    cotangent = normal_values(keys[1], (LENGTH, NSEQ, MODEL_DIMENSION), 1.0, 6.0, ((0, 8), (1, 4)))
    query_key_value_weight = normal_values(keys[2], (MODEL_DIMENSION, QUERY_HEADS * HEAD_SIZE + 2 * KEY_VALUE_HEADS * HEAD_SIZE), MODEL_DIMENSION ** -0.5, 0.1875, ((0, 2),))
    w_o = normal_values(keys[3], (QUERY_HEADS * HEAD_SIZE, MODEL_DIMENSION), 4 ** -0.5, 3.0, ((0, 2),))
    w_gu = normal_values(keys[4], (MODEL_DIMENSION, 2 * FF), MODEL_DIMENSION ** -0.5, 0.1875, ((0, 2),))
    w_down = normal_values(keys[5], (FF, MODEL_DIMENSION), FF ** -0.5, 0.09375, ((0, 2),))
    g_attn = jnp.clip(1.0 + 0.1 * jax.random.normal(keys[6], (MODEL_DIMENSION,), jnp.float32), 0.5, 1.5).astype(jnp.bfloat16)
    g_ffn = jnp.clip(1.0 + 0.1 * jax.random.normal(keys[7], (MODEL_DIMENSION,), jnp.float32), 0.5, 1.5).astype(jnp.bfloat16)
    g_q = jnp.clip(1.0 + 0.1 * jax.random.normal(keys[8], (HEAD_SIZE,), jnp.float32), 0.5, 1.5).astype(jnp.bfloat16)
    key_norm_gain = jnp.clip(1.0 + 0.1 * jax.random.normal(keys[9], (HEAD_SIZE,), jnp.float32), 0.5, 1.5).astype(jnp.bfloat16)
    a_qkv = normal_values(keys[10], (ADAPTER_SETS, MODEL_DIMENSION, 3 * ADAPTER_RANK), MODEL_DIMENSION ** -0.5, 0.1875)
    b_q = normal_values(keys[11], (ADAPTER_SETS, ADAPTER_RANK, QUERY_HEADS * HEAD_SIZE), (4 * ADAPTER_RANK) ** -0.5, 0.75)
    key_up_weight = normal_values(keys[12], (ADAPTER_SETS, ADAPTER_RANK, KEY_VALUE_HEADS * HEAD_SIZE), (4 * ADAPTER_RANK) ** -0.5, 0.75)
    value_up_weight = normal_values(keys[13], (ADAPTER_SETS, ADAPTER_RANK, KEY_VALUE_HEADS * HEAD_SIZE), (4 * ADAPTER_RANK) ** -0.5, 0.75)
    a_o = normal_values(keys[14], (ADAPTER_SETS, QUERY_HEADS * HEAD_SIZE, ADAPTER_RANK), (QUERY_HEADS * HEAD_SIZE) ** -0.5, 0.1875)
    b_o = normal_values(keys[15], (ADAPTER_SETS, ADAPTER_RANK, MODEL_DIMENSION), 1 ** -0.5, 6.0)
    a_gu = normal_values(keys[16], (ADAPTER_SETS, MODEL_DIMENSION, 2 * ADAPTER_RANK), MODEL_DIMENSION ** -0.5, 0.1875)
    b_gu = normal_values(keys[17], (ADAPTER_SETS, 2, ADAPTER_RANK, FF), (4 * ADAPTER_RANK) ** -0.5, 0.75)
    a_down = normal_values(keys[18], (ADAPTER_SETS, FF, ADAPTER_RANK), FF ** -0.5, 0.09375)
    b_down = normal_values(keys[19], (ADAPTER_SETS, ADAPTER_RANK, MODEL_DIMENSION), (4 * ADAPTER_RANK) ** -0.5, 0.75)
    set_index = with_ends(jax.random.randint(keys[20], (NSEQ,), 0, ADAPTER_SETS), jax.random.fold_in(keys[20], 1), 0, ADAPTER_SETS - 1).astype(jnp.int32)
    stretch_order = draw_stretch_order(jax.random.fold_in(keys[22], 71), 0)
    return {"hidden_in": hidden_in, "cotangent": cotangent, "query_key_value_weight": query_key_value_weight, "w_o": w_o, "w_gu": w_gu, "w_down": w_down, "g_attn": g_attn, "g_ffn": g_ffn, "g_q": g_q, "key_norm_gain": key_norm_gain, "a_qkv": a_qkv, "b_q": b_q, "key_up_weight": key_up_weight, "value_up_weight": value_up_weight, "a_o": a_o, "b_o": b_o, "a_gu": a_gu, "b_gu": b_gu, "a_down": a_down, "b_down": b_down, "set_index": set_index, "stretch_order": stretch_order}


epsilon = 1e-05
rope_base = 1000000.0
precise = lax.Precision.HIGHEST

@jax.custom_vjp
def adapter_lowrank(v):
    return lax.optimization_barrier(v.astype(jnp.bfloat16)).astype(jnp.float32)

@jax.custom_vjp
def low_back(v):
    return v

def low_keep(v):
    return (adapter_lowrank(v), None)

def low_pass(kept, grad):
    return (grad,)

def back_keep(v):
    return (v, None)

def back_low(kept, grad):
    return (adapter_lowrank(grad),)
adapter_lowrank.defvjp(low_keep, low_pass)
low_back.defvjp(back_keep, back_low)

def matmul(left, right):
    return jnp.dot(left, right, precision=precise, preferred_element_type=jnp.float32)

def root_mean_square_norm(inputs, gain_vec):
    return inputs * lax.rsqrt(lax.optimization_barrier(jnp.mean(inputs * inputs, axis=-1, keepdims=True)) + epsilon) * gain_vec

def rotary_apply(inputs, position_floats):
    half_width = inputs.shape[-1] // 2
    frequency = jnp.exp(-math.log(rope_base) * 2.0 * jnp.arange(half_width, dtype=jnp.float32) / inputs.shape[-1])
    angle_grid = position_floats[:, None] * frequency[None, :]
    cosine_table = jnp.cos(angle_grid)[:, None, :]
    sine_table = jnp.sin(angle_grid)[:, None, :]
    lower_half = inputs[..., :half_width]
    upper_half = inputs[..., half_width:]
    return jnp.concatenate([lower_half * cosine_table - upper_half * sine_table, upper_half * cosine_table + lower_half * sine_table], axis=-1)

def pick(table, onehot):
    return jnp.tensordot(onehot, table, axes=1, precision=precise)

def attention(query_rows, heads_of_keys, heads_of_values, positions):
    total_length = query_rows.shape[0]
    rows_per_block = math.gcd(total_length, 512)
    heads_per_group = QUERY_HEADS // KEY_VALUE_HEADS
    grouped_queries = query_rows.reshape(total_length // rows_per_block, rows_per_block, KEY_VALUE_HEADS, heads_per_group, HEAD_SIZE)
    pos_blocks = positions.reshape(total_length // rows_per_block, rows_per_block)
    score_scale = 1.0 / math.sqrt(HEAD_SIZE)

    def one_block(block_pair):
        q_block, q_pos = block_pair
        scores = jnp.einsum('qgjd,kgd->gjqk', q_block, heads_of_keys, precision=precise) * score_scale
        scores = low_back(scores)
        allowed = (positions[None, :] <= q_pos[:, None])[None, None]
        scores = jnp.where(allowed, scores, -1e+30)
        row_max = lax.optimization_barrier(jnp.max(scores, axis=-1, keepdims=True))
        weights = jnp.where(allowed, jnp.exp(scores - row_max), 0.0)
        probs = adapter_lowrank(weights / lax.optimization_barrier(jnp.sum(weights, axis=-1, keepdims=True)))
        return jnp.einsum('gjqk,kgd->qgjd', probs, heads_of_values, precision=precise)
    outputs = lax.map(jax.checkpoint(one_block), (grouped_queries, pos_blocks))
    return outputs.reshape(total_length, QUERY_HEADS * HEAD_SIZE)

def layer(inputs, tables, frozen, gains, onehot, positions):
    query_key_value_weight, w_o, w_gu, w_down = frozen
    g_attn, g_ffn, g_q, key_norm_gain = gains
    a_qkv, b_q, key_up_weight, value_up_weight, a_o, b_o, a_gu, b_gu, a_down, b_down = [pick(table, onehot) for table in tables]
    total_length = inputs.shape[0]
    q_width = QUERY_HEADS * HEAD_SIZE
    key_total_width = KEY_VALUE_HEADS * HEAD_SIZE
    normed_attn = adapter_lowrank(root_mean_square_norm(inputs, g_attn))
    rank_qkv = adapter_lowrank(low_back(matmul(normed_attn, a_qkv)))
    joined = matmul(normed_attn, query_key_value_weight)
    q_raw = low_back(joined[:, :q_width] + matmul(rank_qkv[:, :ADAPTER_RANK], b_q))
    key_unnormed = low_back(joined[:, q_width:q_width + key_total_width] + matmul(rank_qkv[:, ADAPTER_RANK:2 * ADAPTER_RANK], key_up_weight))
    value_unnormed = low_back(joined[:, q_width + key_total_width:] + matmul(rank_qkv[:, 2 * ADAPTER_RANK:], value_up_weight))
    position_floats = positions.astype(jnp.float32)
    query_rows = adapter_lowrank(rotary_apply(root_mean_square_norm(q_raw.reshape(total_length, QUERY_HEADS, HEAD_SIZE), g_q), position_floats))
    heads_of_keys = adapter_lowrank(rotary_apply(root_mean_square_norm(key_unnormed.reshape(total_length, KEY_VALUE_HEADS, HEAD_SIZE), key_norm_gain), position_floats))
    heads_of_values = adapter_lowrank(value_unnormed).reshape(total_length, KEY_VALUE_HEADS, HEAD_SIZE)
    attended = adapter_lowrank(low_back(attention(query_rows, heads_of_keys, heads_of_values, positions)))
    rank_o = adapter_lowrank(low_back(matmul(attended, a_o)))
    mixed = low_back(matmul(attended, w_o) + matmul(rank_o, b_o))
    residual = inputs + mixed
    normed_ffn = adapter_lowrank(root_mean_square_norm(residual, g_ffn))
    rank_gu = adapter_lowrank(low_back(matmul(normed_ffn, a_gu)))
    joined_ffn = matmul(normed_ffn, w_gu)
    gate_pre = low_back(joined_ffn[:, :FF] + matmul(rank_gu[:, :ADAPTER_RANK], b_gu[0]))
    up_pre = low_back(joined_ffn[:, FF:] + matmul(rank_gu[:, ADAPTER_RANK:], b_gu[1]))
    hidden = adapter_lowrank(jax.nn.silu(gate_pre) * up_pre)
    rank_down = adapter_lowrank(low_back(matmul(hidden, a_down)))
    down_out = low_back(matmul(hidden, w_down) + matmul(rank_down, b_down))
    return residual + down_out

def reference(hidden_in, cotangent, query_key_value_weight, w_o, w_gu, w_down, g_attn, g_ffn, g_q, key_norm_gain, a_qkv, b_q, key_up_weight, value_up_weight, a_o, b_o, a_gu, b_gu, a_down, b_down, set_index, stretch_order):
    frozen = tuple((weight.astype(jnp.float32) for weight in (query_key_value_weight, w_o, w_gu, w_down)))
    gains = tuple((gain_vec.astype(jnp.float32) for gain_vec in (g_attn, g_ffn, g_q, key_norm_gain)))
    tables = tuple((table.astype(jnp.float32) for table in (a_qkv, b_q, key_up_weight, value_up_weight, a_o, b_o, a_gu, b_gu, a_down, b_down)))
    row_ids = jnp.arange(LENGTH, dtype=jnp.int32)
    set_ids = jnp.arange(ADAPTER_SETS, dtype=jnp.int32)

    def one_sequence(running, item):
        inputs, upstream, which_set, order_row = item
        onehot = (set_ids == which_set).astype(jnp.float32)
        positions = order_row[row_ids // CH] * CH + row_ids % CH

        def forward_fn(values_in, tables_in):
            return layer(values_in, tables_in, frozen, gains, onehot, positions)
        result, pullback = jax.vjp(forward_fn, inputs.astype(jnp.float32), tables)
        grad_in, grad_tables = pullback(upstream.astype(jnp.float32))
        running = tuple((total_now + fresh for total_now, fresh in zip(running, grad_tables)))
        return (running, (result, grad_in))
    initial = tuple((jnp.zeros_like(table) for table in tables))
    sums, (results, grads_in) = lax.scan(one_sequence, initial, (jnp.swapaxes(hidden_in, 0, 1), jnp.swapaxes(cotangent, 0, 1), set_index, stretch_order))
    layer_out = jnp.swapaxes(results, 0, 1)
    input_grad = jnp.swapaxes(grads_in, 0, 1)
    return (layer_out, input_grad, sums[0], sums[1], sums[2], sums[3], sums[4], sums[5], sums[6], sums[7], sums[8], sums[9])
```

```python
import functools
import math

import jax
import jax.numpy as jnp
import numpy as np
from jax import lax
from jax.experimental import pallas as pl
from jax.experimental.pallas import tpu as pltpu
from jax.sharding import PartitionSpec as P

QUERY_HEADS = 16
KEY_VALUE_HEADS = 8
HEAD_SIZE = 64
FF = 4608
ADAPTER_RANK = 16
ADAPTER_SETS = 8
CH = 128

epsilon = 1e-05
rope_base = 1000000.0

TOK = 4 * CH
PAIR = 2 * HEAD_SIZE
QW = QUERY_HEADS * HEAD_SIZE // 2
KW = KEY_VALUE_HEADS * HEAD_SIZE // 2
EW = QW + 2 * KW
GROUPS = KEY_VALUE_HEADS // 2
HF = FF // 2
TF = 256
NT = HF // TF
R = ADAPTER_RANK
VMEM = 56 * 1024 * 1024
f32 = jnp.float32
bf16 = jnp.bfloat16


def mm(a, b):
    return lax.dot_general(a, b, (((1,), (0,)), ((), ())), preferred_element_type=f32)


def mm_nt(a, b):
    return lax.dot_general(a, b, (((1,), (1,)), ((), ())), preferred_element_type=f32)


def params(sem=("arbitrary",)):
    return pltpu.CompilerParams(dimension_semantics=sem, vmem_limit_bytes=VMEM)


def cost(flops, nbytes):
    return pl.CostEstimate(flops=int(flops), bytes_accessed=int(nbytes), transcendentals=0)


def whole(shape):
    return pl.BlockSpec(shape, lambda *_: (0,) * len(shape))


def split_dot(x, ones):
    hi = x.astype(bf16)
    lo = (x - hi.astype(f32)).astype(bf16)
    return mm(hi, ones) + mm(lo, ones)


def head_mean(x, ones):
    width = ones.shape[0]
    parts = [
        split_dot(x[:, i : i + width], ones) for i in range(0, x.shape[1], width)
    ]
    return jnp.concatenate(parts, axis=1) * (1.0 / HEAD_SIZE)


def lane_iota(shape):
    return lax.broadcasted_iota(jnp.int32, shape, len(shape) - 1)


def half_turn(x):
    width = x.shape[1]
    near = pltpu.roll(x, HEAD_SIZE // 2, 1)
    far = pltpu.roll(x, width - HEAD_SIZE // 2, 1)
    return jnp.where(lane_iota(x.shape) % HEAD_SIZE < HEAD_SIZE // 2, far, near)


def widen(table, width):
    return jnp.concatenate([table] * (width // table.shape[1]), axis=1)


def put_masked(x, ref, index):
    left = lane_iota((x.shape[0], PAIR)) < HEAD_SIZE
    for g in range(GROUPS):
        tile = x[:, g * PAIR : (g + 1) * PAIR]
        turned = pltpu.roll(tile, HEAD_SIZE, 1)
        if g % 2 == 0:
            pair = (jnp.where(left, tile, 0.0), jnp.where(left, turned, 0.0))
        else:
            pair = (jnp.where(left, 0.0, turned), jnp.where(left, 0.0, tile))
        for j in range(2):
            index(ref, g, j, pair[j].astype(bf16))


def qkv_kernel(
    sc, mine, other, cos, sin, w_own, w_rec, gain, a_t, b_q, b_k, b_v, g_qk, ones,
    x_out, u_out, raw_out, qm_out, kv_out, u_s, b_s,
):
    core = sc[0]
    blk = pl.program_id(0)
    x = jnp.where(blk == core, mine[...], other[...])
    half = x.shape[0] // 2
    x_out[0, 0] = x[:half]
    x_out[1, 0] = x[half:]
    x = x.astype(f32)
    inv = lax.rsqrt(jnp.mean(x * x, axis=1, keepdims=True) + epsilon)
    u = (x * inv * gain[...]).astype(bf16)
    u_s[...] = u
    u_out[0, 0] = u[:half]
    u_out[1, 0] = u[half:]
    b_s[...] = jnp.zeros_like(b_s)
    b_s[0:R, 0:QW] = b_q[0]
    b_s[R : 2 * R, QW : QW + KW] = b_k[0]
    b_s[2 * R : 3 * R, QW + KW : EW] = b_v[0]
    depth = w_own.shape[0]
    rank = mm_nt(u, a_t[0]).astype(bf16)
    raw = mm(u_s[:, pl.ds(pl.multiple_of(core * depth, depth), depth)], w_own[...])
    raw += mm(u_s[:, pl.ds(pl.multiple_of((1 - core) * depth, depth), depth)], w_rec[...])
    raw += mm(rank, b_s[...])
    qk = raw[:, : QW + KW]
    raw_out[0, 0] = qk[:half]
    raw_out[1, 0] = qk[half:]
    normed = qk * lax.rsqrt(head_mean(qk * qk, ones[...]) + epsilon) * g_qk[...]
    c = jnp.concatenate([cos[0, 0], cos[1, 0]], axis=0)
    s = jnp.concatenate([sin[0, 0], sin[1, 0]], axis=0)
    turned = normed * widen(c, QW + KW) + half_turn(normed) * widen(s, QW + KW)

    def put(ref, g, j, value):
        ref[g, j, 0, 0] = value[:half]
        ref[g, j, 1, 0] = value[half:]

    put_masked(turned[:, :QW] * (1.0 / math.sqrt(HEAD_SIZE)), qm_out, put)
    kv = jnp.concatenate([turned[:, QW:], raw[:, QW + KW :]], axis=1).astype(bf16)
    kv_out[0, 0] = kv[:half]
    kv_out[1, 0] = kv[half:]


def qkv_call(sc, mine, other, cos, sin, w_own, w_rec, gain, a_t, b_q, b_k, b_v, g_qk, ones):
    rows, width = mine.shape
    depth = w_own.shape[0]

    def out(n, dtype):
        return jax.ShapeDtypeStruct((2, 2, CH, n), dtype)

    def out_spec(n):
        return pl.BlockSpec((2, 1, CH, n), lambda i, s: (0, i, 0, 0))

    return pl.pallas_call(
        qkv_kernel,
        grid_spec=pltpu.PrefetchScalarGridSpec(
            num_scalar_prefetch=1,
            grid=(2,),
            in_specs=[
                whole((rows, width)), whole((rows, width)),
                out_spec(PAIR), out_spec(PAIR),
                whole((depth, EW)), whole((depth, EW)),
                whole((1, width)),
                pl.BlockSpec((1, 3 * R, width), lambda i, s: (s[1], 0, 0)),
                pl.BlockSpec((1, R, QW), lambda i, s: (s[1], 0, s[0])),
                pl.BlockSpec((1, R, KW), lambda i, s: (s[1], 0, s[0])),
                pl.BlockSpec((1, R, KW), lambda i, s: (s[1], 0, s[0])),
                whole((1, QW + KW)), whole(ones.shape),
            ],
            out_specs=[
                out_spec(width), out_spec(width), out_spec(QW + KW),
                pl.BlockSpec((GROUPS, 2, 2, 1, CH, PAIR), lambda i, s: (0, 0, 0, i, 0, 0)),
                out_spec(2 * KW),
            ],
            scratch_shapes=[pltpu.VMEM((rows, width), bf16), pltpu.VMEM((3 * R, EW), bf16)],
        ),
        out_shape=[
            out(width, bf16), out(width, bf16), out(QW + KW, f32),
            jax.ShapeDtypeStruct((GROUPS, 2, 2, 2, CH, PAIR), bf16), out(2 * KW, bf16),
        ],
        compiler_params=params(),
        cost_estimate=cost(2 * TOK * width * EW, 8e6),
        name="qkv",
    )(sc, mine, other, cos, sin, w_own, w_rec, gain, a_t, b_q, b_k, b_v, g_qk, ones)


def sub_blocks(sc, base, first):
    out = []
    for qb in range(2):
        for kb in range(2):
            if first and qb == kb:
                out.append((qb * CH, kb * CH, True))
                out.append(((2 + qb) * CH, (2 + kb) * CH, True))
            else:
                flag = sc[base + qb * 2 + kb]
                q_at = pl.multiple_of((1 - flag) * (2 * CH) + qb * CH, CH)
                k_at = pl.multiple_of((1 - flag) * (2 * CH) + kb * CH, CH)
                out.append((q_at, k_at, False))
    return out


def attend_kernel(base, first, sc, qm, k, v, *rest):
    if first:
        acc_out, acc, vx = rest
    else:
        acc_in, acc_out, acc, vx = rest
    g = pl.program_id(0)
    acc[...] = jnp.zeros_like(acc)
    vx[:, :PAIR] = v[...]
    vx[:, PAIR:] = jnp.ones_like(v[...])
    high = 2 * CH

    def part(q_at, q_n, k_at, k_n, diagonal):
        rows = pl.ds(q_at, q_n)
        keys = pl.ds(k_at, k_n)
        q2 = jnp.concatenate([qm[0, 0, rows, :], qm[0, 1, rows, :]], axis=0)
        p = jnp.exp(mm_nt(q2, k[keys, :]))
        if diagonal:
            t = lax.broadcasted_iota(jnp.int32, p.shape, 0) % q_n
            p = jnp.where(lane_iota(p.shape) <= t, p, 0.0)
        o = mm(p.astype(bf16), vx[keys, :])
        acc[0, rows, :] += o[:q_n]
        acc[1, rows, :] += o[q_n:]

    part(high, 2 * CH, 0, 2 * CH, False)
    for q_at, k_at, diagonal in sub_blocks(sc, base, first):
        part(q_at, CH, k_at, CH, diagonal)
    left = lane_iota((TOK, PAIR)) < HEAD_SIZE
    even = g % 2 == 0
    o0, o1 = acc[0, :, :PAIR], acc[1, :, :PAIR]
    o0 = jnp.where(even, o0, pltpu.roll(o0, HEAD_SIZE, 1))
    o1 = jnp.where(even, pltpu.roll(o1, HEAD_SIZE, 1), o1)
    o = jnp.where(left, o0, o1)
    norm = jnp.where(left, acc[0, :, PAIR:], acc[1, :, PAIR:])
    if not first:
        o += acc_in[0, :, :PAIR]
        norm += acc_in[0, :, PAIR:]
    acc_out[0, :, :PAIR] = o
    acc_out[0, :, PAIR:] = norm


def attend_call(base, sc, qm, kv, acc):
    first = acc is None
    acc_spec = pl.BlockSpec((1, TOK, 2 * PAIR), lambda g, s: (g, 0, 0))
    return pl.pallas_call(
        functools.partial(attend_kernel, base, first),
        grid_spec=pltpu.PrefetchScalarGridSpec(
            num_scalar_prefetch=1,
            grid=(GROUPS,),
            in_specs=[
                pl.BlockSpec((1, 2, TOK, PAIR), lambda g, s: (g, 0, 0, 0)),
                pl.BlockSpec((TOK, PAIR), lambda g, s: (0, g // 2)),
                pl.BlockSpec((TOK, PAIR), lambda g, s: (0, GROUPS // 2 + g // 2)),
            ]
            + ([] if first else [acc_spec]),
            out_specs=acc_spec,
            scratch_shapes=[
                pltpu.VMEM((2, TOK, 2 * PAIR), f32),
                pltpu.VMEM((TOK, 2 * PAIR), bf16),
            ],
        ),
        out_shape=jax.ShapeDtypeStruct((GROUPS, TOK, 2 * PAIR), f32),
        input_output_aliases={} if first else {4: 0},
        compiler_params=params(),
        cost_estimate=cost(2.4e9, 5e6),
        name="attend",
    )(sc, qm, kv, kv, *([] if first else [acc]))


def project_kernel(sc, acc, w_o, a_o, b_o, pick, ob_out, mix_out, lse_out):
    o = jnp.concatenate([acc[g, :, :PAIR] / acc[g, :, PAIR:] for g in range(GROUPS)], axis=1)
    ob = o.astype(bf16)
    ob_out[...] = ob
    norm = jnp.concatenate([acc[g, :, PAIR:] for g in range(GROUPS)], axis=1)
    lse_out[...] = lax.dot_general(
        pick[...], jnp.log(norm), (((1,), (1,)), ((), ())),
        precision=lax.Precision.HIGHEST, preferred_element_type=f32,
    )
    rank = mm_nt(ob, a_o[0]).astype(bf16)
    mix_out[...] = (mm(ob, w_o[...]) + mm(rank, b_o[0])).astype(bf16)


def project_call(sc, acc, w_o, a_o, b_o, pick):
    width = w_o.shape[1]
    return pl.pallas_call(
        project_kernel,
        grid_spec=pltpu.PrefetchScalarGridSpec(
            num_scalar_prefetch=1,
            grid=(1,),
            in_specs=[
                whole(acc.shape), whole(w_o.shape),
                pl.BlockSpec((1, R, QW), lambda i, s: (s[1], 0, s[0])),
                pl.BlockSpec((1, R, width), lambda i, s: (s[1], 0, 0)),
                whole(pick.shape),
            ],
            out_specs=[whole((TOK, QW)), whole((TOK, width)), whole((2 * GROUPS, TOK))],
        ),
        out_shape=[
            jax.ShapeDtypeStruct((TOK, QW), bf16),
            jax.ShapeDtypeStruct((TOK, width), bf16),
            jax.ShapeDtypeStruct((2 * GROUPS, TOK), f32),
        ],
        compiler_params=params(),
        cost_estimate=cost(2 * TOK * QW * width, 6e6),
        name="project",
    )(sc, acc, w_o, a_o, b_o, pick)


def ffn_kernel(
    sc, x, mix_a, mix_b, ed, gain, wg_own, wu_own, wg_rec, wu_rec, w_d, a_gu, b_gu, a_d, b_d,
    h_out, down_out, du_out, gb_gu, ga_d, gb_d, ga_gu,
    u_s, down_s, du_s, rgu_s, rguT_s, drd_s, drdT_s, rd_s, drgu_s,
):
    i = pl.program_id(0)
    core = sc[0]
    depth = wg_own.shape[0]
    own = pl.ds(pl.multiple_of(core * depth, depth), depth)
    rec = pl.ds(pl.multiple_of((1 - core) * depth, depth), depth)

    @pl.when(i == 0)
    def _():
        h = x[...].astype(f32) + (mix_a[...].astype(f32) + mix_b[...].astype(f32))
        h_out[...] = h
        inv = lax.rsqrt(jnp.mean(h * h, axis=1, keepdims=True) + epsilon)
        u = (h * inv * gain[...]).astype(bf16)
        u_s[...] = u
        rgu_s[...] = mm_nt(u, a_gu[0]).astype(bf16)
        rguT_s[...] = mm_nt(a_gu[0], u).astype(bf16)
        drd_s[...] = mm_nt(ed[...], b_d[0]).astype(bf16)
        drdT_s[...] = mm_nt(b_d[0], ed[...]).astype(bf16)
        down_s[...] = jnp.zeros_like(down_s)
        du_s[...] = jnp.zeros_like(du_s)
        rd_s[...] = jnp.zeros_like(rd_s)
        drgu_s[...] = jnp.zeros_like(drgu_s)

    u_own, u_rec = u_s[:, own], u_s[:, rec]
    gate = mm(u_own, wg_own[...]) + mm(u_rec, wg_rec[...]) + mm(rgu_s[:, :R], b_gu[0, 0])
    up = mm(u_own, wu_own[...]) + mm(u_rec, wu_rec[...]) + mm(rgu_s[:, R:], b_gu[0, 1])
    d_hid = mm_nt(ed[...], w_d[...]) + mm(drd_s[...], a_d[0])
    sig = jax.nn.sigmoid(gate)
    silu = gate * sig
    hid = (silu * up).astype(bf16)
    e_g = (d_hid * up * (sig * (1.0 + gate * (1.0 - sig)))).astype(bf16)
    e_u = (d_hid * silu).astype(bf16)
    down_s[...] += mm(hid, w_d[...])
    rd_s[...] += mm_nt(hid, a_d[0])
    du_s[:, own] += mm_nt(e_g, wg_own[...]) + mm_nt(e_u, wu_own[...])
    du_s[:, rec] += mm_nt(e_g, wg_rec[...]) + mm_nt(e_u, wu_rec[...])
    drgu_s[:, :R] += mm_nt(e_g, b_gu[0, 0])
    drgu_s[:, R:] += mm_nt(e_u, b_gu[0, 1])
    gb_gu[0] = mm(rguT_s[:R], e_g).astype(bf16)
    gb_gu[1] = mm(rguT_s[R:], e_u).astype(bf16)
    ga_d[...] = mm(drdT_s[...], hid).astype(bf16)

    @pl.when(i == pl.num_programs(0) - 1)
    def _():
        rd = rd_s[...].astype(bf16)
        down_out[...] = (down_s[...] + mm(rd, b_d[0])).astype(bf16)
        gb_d[...] = mm(rd_s[...].T.astype(bf16), ed[...]).astype(bf16)
        dr = drgu_s[...].astype(bf16)
        du_out[...] = (du_s[...] + mm(dr, a_gu[0])).astype(bf16)
        ga_gu[...] = mm(drgu_s[...].T.astype(bf16), u_s[...]).astype(bf16)


def ffn_call(sc, x, mix_a, mix_b, ed, gain, w_gu, w_rec, w_d, a_gu, b_gu, a_d, b_d):
    width = x.shape[1]
    depth = w_gu.shape[0]
    return pl.pallas_call(
        ffn_kernel,
        grid_spec=pltpu.PrefetchScalarGridSpec(
            num_scalar_prefetch=1,
            grid=(NT,),
            in_specs=[
                whole((TOK, width)), whole((TOK, width)), whole((TOK, width)), whole((TOK, width)),
                whole((1, width)),
                pl.BlockSpec((depth, TF), lambda i, s: (0, s[0] * NT + i)),
                pl.BlockSpec((depth, TF), lambda i, s: (0, 2 * NT + s[0] * NT + i)),
                pl.BlockSpec((depth, TF), lambda i, s: (0, i)),
                pl.BlockSpec((depth, TF), lambda i, s: (0, NT + i)),
                pl.BlockSpec((TF, width), lambda i, s: (i, 0)),
                pl.BlockSpec((1, 2 * R, width), lambda i, s: (s[1], 0, 0)),
                pl.BlockSpec((1, 2, R, TF), lambda i, s: (s[1], 0, 0, s[0] * NT + i)),
                pl.BlockSpec((1, R, TF), lambda i, s: (s[1], 0, s[0] * NT + i)),
                pl.BlockSpec((1, R, width), lambda i, s: (s[1], 0, 0)),
            ],
            out_specs=[
                whole((TOK, width)), whole((TOK, width)), whole((TOK, width)),
                pl.BlockSpec((2, R, TF), lambda i, s: (0, 0, i)),
                pl.BlockSpec((R, TF), lambda i, s: (0, i)),
                whole((R, width)), whole((2 * R, width)),
            ],
            scratch_shapes=[
                pltpu.VMEM((TOK, width), bf16),
                pltpu.VMEM((TOK, width), f32),
                pltpu.VMEM((TOK, width), f32),
                pltpu.VMEM((TOK, 2 * R), bf16),
                pltpu.VMEM((2 * R, TOK), bf16),
                pltpu.VMEM((TOK, R), bf16),
                pltpu.VMEM((R, TOK), bf16),
                pltpu.VMEM((TOK, R), f32),
                pltpu.VMEM((TOK, 2 * R), f32),
            ],
        ),
        out_shape=[
            jax.ShapeDtypeStruct((TOK, width), f32),
            jax.ShapeDtypeStruct((TOK, width), bf16),
            jax.ShapeDtypeStruct((TOK, width), bf16),
            jax.ShapeDtypeStruct((2, R, HF), bf16),
            jax.ShapeDtypeStruct((R, HF), bf16),
            jax.ShapeDtypeStruct((R, width), bf16),
            jax.ShapeDtypeStruct((2 * R, width), bf16),
        ],
        compiler_params=params(),
        cost_estimate=cost(2 * TOK * HF * width * 6, 2.5e7),
        name="ffn",
    )(sc, x, mix_a, mix_b, ed, gain, w_gu, w_gu, w_rec, w_rec, w_d, a_gu, b_gu, a_d, b_d)


def back_mix_kernel(
    sc, h, ed, du_a, du_b, gain, w_o, a_o, b_o, acc, ob, pick,
    dh_out, dom_out, delta_out, gb_o, ga_o,
):
    hv = h[...]
    inv = lax.rsqrt(jnp.mean(hv * hv, axis=1, keepdims=True) + epsilon)
    w = gain[...] * (du_a[...].astype(f32) + du_b[...].astype(f32))
    dh = ed[...].astype(f32) + inv * w - hv * (
        inv * inv * inv * jnp.mean(hv * w, axis=1, keepdims=True)
    )
    dh_out[...] = dh
    e_o = dh.astype(bf16)
    dr = mm_nt(e_o, b_o[0]).astype(bf16)
    drT = mm_nt(b_o[0], e_o).astype(bf16)
    rT = mm_nt(a_o[0], ob[...]).astype(bf16)
    gb_o[...] = mm(rT, e_o).astype(bf16)
    ga_o[...] = mm(drT, ob[...]).astype(bf16)
    d_o = (mm_nt(e_o, w_o[...]) + mm(dr, a_o[0])).astype(bf16).astype(f32)
    o = jnp.concatenate([acc[g, :, :PAIR] / acc[g, :, PAIR:] for g in range(GROUPS)], axis=1)
    delta_out[...] = lax.dot_general(
        pick[...], d_o * o, (((1,), (1,)), ((), ())),
        precision=lax.Precision.HIGHEST, preferred_element_type=f32,
    )

    def put(ref, g, j, value):
        ref[g, j] = value

    put_masked(d_o, dom_out, put)


def back_mix_call(sc, h, ed, du_a, du_b, gain, w_o, a_o, b_o, acc, ob, pick):
    width = h.shape[1]
    return pl.pallas_call(
        back_mix_kernel,
        grid_spec=pltpu.PrefetchScalarGridSpec(
            num_scalar_prefetch=1,
            grid=(1,),
            in_specs=[
                whole((TOK, width)), whole((TOK, width)), whole((TOK, width)), whole((TOK, width)),
                whole((1, width)), whole(w_o.shape),
                pl.BlockSpec((1, R, QW), lambda i, s: (s[1], 0, s[0])),
                pl.BlockSpec((1, R, width), lambda i, s: (s[1], 0, 0)),
                whole(acc.shape), whole(ob.shape), whole(pick.shape),
            ],
            out_specs=[
                whole((TOK, width)), whole((GROUPS, 2, TOK, PAIR)), whole((2 * GROUPS, TOK)),
                whole((R, width)), whole((R, QW)),
            ],
        ),
        out_shape=[
            jax.ShapeDtypeStruct((TOK, width), f32),
            jax.ShapeDtypeStruct((GROUPS, 2, TOK, PAIR), bf16),
            jax.ShapeDtypeStruct((2 * GROUPS, TOK), f32),
            jax.ShapeDtypeStruct((R, width), bf16),
            jax.ShapeDtypeStruct((R, QW), bf16),
        ],
        compiler_params=params(),
        cost_estimate=cost(2 * TOK * QW * width, 1.2e7),
        name="back_mix",
    )(sc, h, ed, du_a, du_b, gain, w_o, a_o, b_o, acc, ob, pick)


def attend_back_kernel(base, first, has_dq, sc, qm, dom, k, v, lse, delta, *rest):
    if has_dq:
        dq_in, dq_out, dk_out, dv_out, dq, dk, dv, kt = rest
    else:
        dq_out, dk_out, dv_out, dq, dk, dv, kt = rest
    g = pl.program_id(0)
    side = g % 2
    dq[...] = jnp.zeros_like(dq)

    @pl.when(side == 0)
    def _():
        dk[...] = jnp.zeros_like(dk)
        dv[...] = jnp.zeros_like(dv)
        kt[...] = k[...].astype(f32).T.astype(bf16)

    kth = kt.at[pl.ds(pl.multiple_of(side * HEAD_SIZE, HEAD_SIZE), HEAD_SIZE), :]

    def part(q_at, q_n, k_at, k_n, diagonal):
        rows = pl.ds(q_at, q_n)
        keys = pl.ds(k_at, k_n)

        def both(ref):
            return jnp.concatenate([ref[0, 0, rows, :], ref[0, 1, rows, :]], axis=0)

        def line(ref):
            return jnp.concatenate([ref[0, 0:1, rows], ref[0, 1:2, rows]], axis=1)

        q2, do2 = both(qm), both(dom)
        s = mm_nt(k[keys, :], q2)
        p = jnp.exp(s - line(lse))
        if diagonal:
            t = lane_iota(p.shape) % q_n
            p = jnp.where(lax.broadcasted_iota(jnp.int32, p.shape, 0) <= t, p, 0.0)
        dp = mm_nt(v[keys, :], do2)
        ds = (p * (dp - line(delta))).astype(bf16)
        dv[keys, :] += mm(p.astype(bf16), do2)
        dk[keys, :] += mm(ds, q2)
        dqp = mm(kth[:, keys], ds)
        dq[0, :, rows] += dqp[:, :q_n]
        dq[1, :, rows] += dqp[:, q_n:]

    part(2 * CH, 2 * CH, 0, 2 * CH, False)
    for q_at, k_at, diagonal in sub_blocks(sc, base, first):
        part(q_at, CH, k_at, CH, diagonal)
    if has_dq:
        dq_out[0] = dq_in[0] + dq[...]
    else:
        dq_out[0] = dq[...]

    @pl.when(side == 1)
    def _():
        dk_out[...] = dk[...].astype(dk_out.dtype)
        dv_out[...] = dv[...].astype(dv_out.dtype)


def attend_back_call(base, first, sc, qm, dom, kv, lse, delta, dq):
    has_dq = dq is not None
    kind = f32 if first else bf16
    dq_spec = pl.BlockSpec((1, 2, HEAD_SIZE, TOK), lambda g, s: (g, 0, 0, 0))
    row_spec = pl.BlockSpec((1, 2, TOK), lambda g, s: (g, 0, 0))
    pair_spec = pl.BlockSpec((TOK, PAIR), lambda g, s: (0, g // 2))
    return pl.pallas_call(
        functools.partial(attend_back_kernel, base, first, has_dq),
        grid_spec=pltpu.PrefetchScalarGridSpec(
            num_scalar_prefetch=1,
            grid=(GROUPS,),
            in_specs=[
                pl.BlockSpec((1, 2, TOK, PAIR), lambda g, s: (g, 0, 0, 0)),
                pl.BlockSpec((1, 2, TOK, PAIR), lambda g, s: (g, 0, 0, 0)),
                pair_spec,
                pl.BlockSpec((TOK, PAIR), lambda g, s: (0, GROUPS // 2 + g // 2)),
                row_spec, row_spec,
            ]
            + ([dq_spec] if has_dq else []),
            out_specs=[dq_spec, pair_spec, pair_spec],
            scratch_shapes=[
                pltpu.VMEM((2, HEAD_SIZE, TOK), f32),
                pltpu.VMEM((TOK, PAIR), f32),
                pltpu.VMEM((TOK, PAIR), f32),
                pltpu.VMEM((PAIR, TOK), bf16),
            ],
        ),
        out_shape=[
            jax.ShapeDtypeStruct((GROUPS, 2, HEAD_SIZE, TOK), f32),
            jax.ShapeDtypeStruct((TOK, KW), kind),
            jax.ShapeDtypeStruct((TOK, KW), kind),
        ],
        input_output_aliases={7: 0} if has_dq else {},
        compiler_params=params(),
        cost_estimate=cost(6e9, 6e6),
        name="attend_back",
    )(sc, qm, dom, kv, kv, lse, delta, *([dq] if has_dq else []))


def qkv_back_kernel(
    parts, sc, dq, dk, dv, *rest
):
    got = rest[: 2 * parts]
    (raw, cos, sin, g_qk, ones, u, w_own, w_rec, a_t, b_q, b_k, b_v,
     du_out, ga_out, gb_out, e_s, b_s) = rest[2 * parts :]
    core = sc[0]
    d_q = dq[...].T * (1.0 / math.sqrt(HEAD_SIZE))
    d_k, d_v = dk[...], dv[...]
    for n in range(parts):
        d_k = d_k + got[2 * n][...].astype(f32)
        d_v = d_v + got[2 * n + 1][...].astype(f32)
    grad = jnp.concatenate([d_q, d_k], axis=1)
    width = QW + KW
    grad = grad * widen(cos[...], width) - half_turn(grad) * widen(sin[...], width)
    v = raw[...]
    inv = lax.rsqrt(head_mean(v * v, ones[...]) + epsilon)
    w = grad * g_qk[...]
    grad = inv * w - v * (inv * inv * inv) * head_mean(v * w, ones[...])
    e_s[:, :width] = grad.astype(bf16)
    e_s[:, width:] = d_v.astype(bf16)
    b_s[...] = jnp.zeros_like(b_s)
    b_s[0:R, 0:QW] = b_q[0]
    b_s[R : 2 * R, QW:width] = b_k[0]
    b_s[2 * R : 3 * R, width:EW] = b_v[0]
    e = e_s[...]
    dr = mm_nt(e, b_s[...]).astype(bf16)
    drT = mm_nt(b_s[...], e).astype(bf16)
    rT = mm_nt(a_t[0], u[...]).astype(bf16)
    gb = mm(rT, e).astype(bf16)
    gb_out[...] = jnp.concatenate(
        [gb[0:R, 0:QW], gb[R : 2 * R, QW:width], gb[2 * R : 3 * R, width:EW]], axis=1
    )
    ga_out[...] = mm(drT, u[...]).astype(bf16)
    du_out[...] = mm(dr, a_t[0])
    depth = w_own.shape[0]
    du_out[:, pl.ds(pl.multiple_of(core * depth, depth), depth)] += mm_nt(e, w_own[...])
    du_out[:, pl.ds(pl.multiple_of((1 - core) * depth, depth), depth)] += mm_nt(e, w_rec[...])


def qkv_back_call(sc, dq, dk, dv, got, raw, cos, sin, g_qk, ones, u, w_own, w_rec, a_t, b_q, b_k, b_v):
    width = u.shape[1]
    depth = w_own.shape[0]
    parts = len(got) // 2
    return pl.pallas_call(
        functools.partial(qkv_back_kernel, parts),
        grid_spec=pltpu.PrefetchScalarGridSpec(
            num_scalar_prefetch=1,
            grid=(1,),
            in_specs=[whole(dq.shape), whole(dk.shape), whole(dv.shape)]
            + [whole(dk.shape)] * (2 * parts)
            + [
                whole(raw.shape), whole(cos.shape), whole(sin.shape), whole(g_qk.shape),
                whole(ones.shape), whole(u.shape), whole(w_own.shape), whole(w_rec.shape),
                pl.BlockSpec((1, 3 * R, width), lambda i, s: (s[1], 0, 0)),
                pl.BlockSpec((1, R, QW), lambda i, s: (s[1], 0, s[0])),
                pl.BlockSpec((1, R, KW), lambda i, s: (s[1], 0, s[0])),
                pl.BlockSpec((1, R, KW), lambda i, s: (s[1], 0, s[0])),
            ],
            out_specs=[whole((TOK, width)), whole((3 * R, width)), whole((R, EW))],
            scratch_shapes=[pltpu.VMEM((TOK, EW), bf16), pltpu.VMEM((3 * R, EW), bf16)],
        ),
        out_shape=[
            jax.ShapeDtypeStruct((TOK, width), f32),
            jax.ShapeDtypeStruct((3 * R, width), bf16),
            jax.ShapeDtypeStruct((R, EW), bf16),
        ],
        compiler_params=params(),
        cost_estimate=cost(2 * TOK * EW * width, 1.2e7),
        name="qkv_back",
    )(sc, dq, dk, dv, *got, raw, cos, sin, g_qk, ones, u, w_own, w_rec, a_t, b_q, b_k, b_v)


def rope_parts():
    freq = np.exp(-math.log(rope_base) * 2.0 * np.arange(HEAD_SIZE // 2) / HEAD_SIZE)
    angle = np.arange(CH)[:, None] * freq[None, :]
    return freq, np.cos(angle).astype(np.float32), np.sin(angle).astype(np.float32)


def rope_tables(stretches):
    freq, cos_t, sin_t = rope_parts()
    angle = (stretches.astype(f32) * CH)[:, None] * jnp.asarray(freq.astype(np.float32))[None, :]
    cos_a, sin_a = jnp.cos(angle)[:, None, :], jnp.sin(angle)[:, None, :]
    cos = cos_a * cos_t[None] - sin_a * sin_t[None]
    sin = sin_a * cos_t[None] + cos_a * sin_t[None]
    return (
        jnp.concatenate([cos, cos, cos, cos], axis=-1),
        jnp.concatenate([-sin, sin, -sin, sin], axis=-1),
    )


def per_device(
    hidden_in, cotangent, query_key_value_weight, w_o, w_gu, w_down, g_attn, g_ffn, g_q,
    key_norm_gain, a_qkv, b_q, key_up_weight, value_up_weight, a_o, b_o, a_gu, b_gu, a_down,
    b_down, set_index, stretch_order,
):
    rows, _, width = hidden_in.shape
    n_ctx = lax.axis_size("ctx")
    n_seq = lax.axis_size("seq")
    half = n_ctx // 2
    core = lax.axis_index("wsh")
    ctx = lax.axis_index("ctx")
    side = ctx // half
    place = ctx % half
    stays = core == side

    def line(s, p, c):
        return (s * half + p) * 2 + c

    swap_pairs = [
        (line(s, p, c), line(c, p, s))
        for s in range(2) for p in range(half) for c in range(2) if s != c
    ]
    core_pairs = [(0, 1), (1, 0)]

    def swap(v):
        return lax.ppermute(v, ("ctx", "wsh"), swap_pairs)

    def other_core(v):
        return lax.ppermute(v, "wsh", core_pairs)

    def partner(v, k):
        return lax.ppermute(
            v, "ctx", [(s * half + p, s * half + (p ^ k)) for s in range(2) for p in range(half)]
        )

    hid = hidden_in.reshape(rows, width)
    cot = cotangent.reshape(rows, width)
    mine = jnp.where(stays, hid, swap(hid))
    order = jnp.where(stays, stretch_order[0], swap(stretch_order)[0])
    other = other_core(mine)
    cot_mine = jnp.where(stays, cot, swap(cot))
    cot_other = other_core(cot_mine)

    def cols(w, start, size, which):
        return lax.dynamic_slice_in_dim(w, start + which * size, size, 1)

    q_all, k_all = 2 * QW, 2 * KW

    def qkv_cols(which):
        return jnp.concatenate(
            [
                cols(query_key_value_weight, 0, QW, which),
                cols(query_key_value_weight, q_all, KW, which),
                cols(query_key_value_weight, q_all + k_all, KW, which),
            ],
            axis=1,
        )

    w_own = qkv_cols(core)
    w_rec = other_core(qkv_cols(1 - core))
    gu_rec = other_core(
        jnp.concatenate([cols(w_gu, 0, HF, 1 - core), cols(w_gu, FF, HF, 1 - core)], axis=1)
    )

    own_set = lax.dynamic_index_in_dim(set_index, lax.axis_index("seq") * 2 + side, keepdims=False)
    low = order.reshape(2, half, 2)
    here = lax.dynamic_index_in_dim(low, place, 1, keepdims=False)
    flags = []
    for k in range(half):
        there = lax.dynamic_index_in_dim(low, place ^ k, 1, keepdims=False)
        flags.append((there[None, :, 0] < here[:, None, 0]).astype(jnp.int32).reshape(4))
    sc = jnp.concatenate([jnp.stack([core, own_set]).astype(jnp.int32)] + flags)
    cos, sin = rope_tables(here.T.reshape(4))
    ones = jnp.asarray(np.kron(np.eye(4), np.ones((HEAD_SIZE, HEAD_SIZE))), bf16)
    pick_one = np.zeros((2 * GROUPS, QW), np.float32)
    pick_sum = np.zeros((2 * GROUPS, QW), np.float32)
    for head in range(2 * GROUPS):
        pick_one[head, head * HEAD_SIZE] = 1.0
        pick_sum[head, head * HEAD_SIZE : (head + 1) * HEAD_SIZE] = 1.0
    gain_a = g_attn.astype(f32)[None]
    gain_f = g_ffn.astype(f32)[None]
    g_qk = jnp.concatenate(
        [jnp.tile(g_q, QW // HEAD_SIZE), jnp.tile(key_norm_gain, KW // HEAD_SIZE)]
    ).astype(f32)[None]
    a_qkv_t = jnp.swapaxes(a_qkv, 1, 2)
    a_o_t = jnp.swapaxes(a_o, 1, 2)
    a_gu_t = jnp.swapaxes(a_gu, 1, 2)
    a_down_t = jnp.swapaxes(a_down, 1, 2)

    four = (2, 2, CH)
    x4, u4, raw4, qm6, kv4 = qkv_call(
        sc, mine, other, cos.reshape(four + (PAIR,)), sin.reshape(four + (PAIR,)), w_own, w_rec,
        gain_a, a_qkv_t, b_q, key_up_weight, value_up_weight, g_qk, ones,
    )
    x = x4.reshape(TOK, width)
    u = u4.reshape(TOK, width)
    raw = raw4.reshape(TOK, QW + KW)
    qm = qm6.reshape(GROUPS, 2, TOK, PAIR)
    kv = kv4.reshape(TOK, 2 * KW)
    kvs = [kv] + [partner(kv, k) for k in range(1, half)]
    acc = None
    for k in range(half):
        acc = attend_call(2 + 4 * k, sc, qm, kvs[k], acc)
    ob, mix, lse = project_call(sc, acc, w_o, a_o_t, b_o, jnp.asarray(pick_one))

    def both(m, o):
        pair = jnp.stack([jnp.where(core == 0, m, o), jnp.where(core == 0, o, m)])
        return jnp.swapaxes(pair.reshape(2, 2, CH, width), 0, 1).reshape(TOK, width)

    ed = both(cot_mine, cot_other)
    h, down, du, gb_gu, ga_d, gb_d, ga_gu = ffn_call(
        sc, x, mix, other_core(mix), ed, gain_f, w_gu, gu_rec, w_down, a_gu_t, b_gu, a_down_t,
        b_down,
    )
    dh, dom, delta, gb_o, ga_o = back_mix_call(
        sc, h, ed, du, other_core(du), gain_f, w_o, a_o_t, b_o, acc, ob, jnp.asarray(pick_sum)
    )
    lse = lse.reshape(GROUPS, 2, TOK)
    delta = delta.reshape(GROUPS, 2, TOK)
    dq = None
    got = []
    for k in list(range(1, half)) + [0]:
        dq, dk, dv = attend_back_call(2 + 4 * k, k == 0, sc, qm, dom, kvs[k], lse, delta, dq)
        if k:
            got += [partner(dk, k), partner(dv, k)]
    du1, ga_qkv, gb_qkv = qkv_back_call(
        sc, dq.reshape(QW, TOK), dk, dv, got, raw, cos.reshape(TOK, PAIR), sin.reshape(TOK, PAIR),
        g_qk, ones, u, w_own, w_rec, a_qkv_t, b_q, key_up_weight, value_up_weight,
    )

    def block_of(v, which):
        v = v.reshape(2, 2, CH, v.shape[1])
        return lax.dynamic_index_in_dim(v, which, 1, keepdims=False).reshape(rows, v.shape[3])

    def home(v):
        back = swap(v.astype(bf16)).astype(f32)
        return jnp.where(stays, v, back).reshape(rows, 1, width)

    down_got = other_core(block_of(down, 1 - core)).astype(f32)
    layer_out = home(block_of(h, core) + (block_of(down, core).astype(f32) + down_got))
    du_got = other_core(block_of(du1, 1 - core).astype(bf16)).astype(f32)
    d_u = block_of(du1, core) + du_got
    xin = mine.astype(f32)
    inv = lax.rsqrt(jnp.mean(xin * xin, axis=1, keepdims=True) + epsilon)
    w = d_u * gain_a
    grad_in = block_of(dh, core) + inv * w - xin * inv**3 * jnp.mean(xin * w, axis=1, keepdims=True)
    input_grad = home(grad_in)

    shared = jnp.concatenate([gb_d, ga_gu, gb_o, ga_qkv], axis=0)
    shared = shared.astype(f32) + other_core(shared).astype(f32)
    n_shared = shared.shape[0] // 2
    shared = lax.dynamic_slice_in_dim(shared, core * n_shared, n_shared, 0).astype(bf16)
    pieces = [shared, gb_gu, ga_d, ga_o, gb_qkv]
    sizes = [p.size for p in pieces]
    flat = jnp.concatenate([p.reshape(-1) for p in pieces]).reshape(half, -1, 128)
    total = lax.dynamic_index_in_dim(flat, place, 0, keepdims=False).astype(f32)
    for k in range(1, half):
        sent = lax.dynamic_index_in_dim(flat, place ^ k, 0, keepdims=False)
        total += partner(sent, k).astype(f32)
    shard = total.astype(bf16)
    spread = [shard] + [partner(shard, k) for k in range(1, half)]
    spread = jnp.stack(spread)
    spread = jnp.concatenate(
        [lax.dynamic_index_in_dim(spread, place ^ p, 0) for p in range(half)]
    )
    side_pairs = [(i, (i + half) % n_ctx) for i in range(n_ctx)]
    spread = jnp.stack([spread, lax.ppermute(spread, "ctx", side_pairs)])
    spread = jnp.stack([lax.dynamic_index_in_dim(spread, side ^ s, 0, keepdims=False) for s in range(2)])
    lines = [spread]
    for k in range(1, n_seq):
        lines.append(lax.ppermute(spread, "seq", [(i, i ^ k) for i in range(n_seq)]))
    lines = jnp.stack(lines)
    seq_at = lax.axis_index("seq")
    lines = jnp.concatenate([lax.dynamic_index_in_dim(lines, seq_at ^ s, 0) for s in range(n_seq)])
    lines = lines.reshape(2 * n_seq, -1)
    twin = other_core(lines)
    cores = (jnp.where(core == 0, lines, twin), jnp.where(core == 0, twin, lines))
    onehot = (set_index[None, :] == jnp.arange(ADAPTER_SETS, dtype=jnp.int32)[:, None]).astype(f32)

    def place_sets(v):
        v = v.astype(f32)
        shape = (ADAPTER_SETS,) + (1,) * (v.ndim - 1)
        out = onehot[:, 0].reshape(shape) * v[0][None]
        for n in range(1, v.shape[0]):
            out += onehot[:, n].reshape(shape) * v[n][None]
        return out

    def piece(which, shape):
        start = sum(sizes[:which])
        return [c[:, start : start + sizes[which]].reshape((2 * n_seq,) + shape) for c in cores]

    sh = place_sets(jnp.concatenate(piece(0, (n_shared, width)), axis=1))
    r_gu = place_sets(jnp.concatenate(piece(1, (2, R, HF)), axis=3))
    r_ad = place_sets(jnp.concatenate(piece(2, (R, HF)), axis=2))
    r_ao = place_sets(jnp.concatenate(piece(3, (R, QW)), axis=2))
    qkv0, qkv1 = piece(4, (R, EW))
    r_bq = place_sets(jnp.concatenate([qkv0[..., :QW], qkv1[..., :QW]], axis=2))
    r_bk = place_sets(jnp.concatenate([qkv0[..., QW : QW + KW], qkv1[..., QW : QW + KW]], axis=2))
    r_bv = place_sets(jnp.concatenate([qkv0[..., QW + KW :], qkv1[..., QW + KW :]], axis=2))
    return (
        layer_out,
        input_grad,
        jnp.swapaxes(sh[:, 4 * R :], 1, 2),
        r_bq,
        r_bk,
        r_bv,
        jnp.swapaxes(r_ao, 1, 2),
        sh[:, 3 * R : 4 * R],
        jnp.swapaxes(sh[:, R : 3 * R], 1, 2),
        r_gu,
        jnp.swapaxes(r_ad, 1, 2),
        sh[:, :R],
    )


def solution(mesh):
    tokens = P("ctx", ("seq", "wsh"), None)
    in_specs = (
        (tokens, tokens) + (P("wsh", None),) * 4 + (P(),) * 15 + (P(("seq", "wsh"), None),)
    )
    out_specs = (tokens, tokens) + (P(),) * 10
    return jax.shard_map(
        per_device, mesh=mesh, in_specs=in_specs, out_specs=out_specs, check_vma=False
    )
```

```python
import functools
import math

import jax
import jax.numpy as jnp
import numpy as np
from jax import lax
from jax.experimental import pallas as pl
from jax.experimental.pallas import tpu as pltpu
from jax.sharding import PartitionSpec as P

QUERY_HEADS = 16
KEY_VALUE_HEADS = 8
HEAD_SIZE = 64
FF = 4608
ADAPTER_RANK = 16
ADAPTER_SETS = 8
CH = 128

epsilon = 1e-05
rope_base = 1000000.0

TOK = 4 * CH
PAIR = 2 * HEAD_SIZE
QW = QUERY_HEADS * HEAD_SIZE // 2
KW = KEY_VALUE_HEADS * HEAD_SIZE // 2
EW = QW + 2 * KW
GROUPS = KEY_VALUE_HEADS // 2
HF = FF // 2
TF = 768
NT = HF // TF
R = ADAPTER_RANK
MIB = 1024 * 1024
f32 = jnp.float32
bf16 = jnp.bfloat16


def mm(a, b):
    return lax.dot_general(a, b, (((1,), (0,)), ((), ())), preferred_element_type=f32)


def mm_nt(a, b):
    return lax.dot_general(a, b, (((1,), (1,)), ((), ())), preferred_element_type=f32)


def params(mib):
    return pltpu.CompilerParams(
        dimension_semantics=("arbitrary",), vmem_limit_bytes=mib * MIB
    )


def cost(flops, nbytes):
    return pl.CostEstimate(flops=int(flops), bytes_accessed=int(nbytes), transcendentals=0)


def whole(shape):
    return pl.BlockSpec(shape, lambda *_: (0,) * len(shape))


def split_dot(x, ones):
    hi = x.astype(bf16)
    lo = (x - hi.astype(f32)).astype(bf16)
    return mm(hi, ones) + mm(lo, ones)


def head_mean(x, ones):
    width = ones.shape[0]
    parts = [
        split_dot(x[:, i : i + width], ones) for i in range(0, x.shape[1], width)
    ]
    return jnp.concatenate(parts, axis=1) * (1.0 / HEAD_SIZE)


def lane_iota(shape):
    return lax.broadcasted_iota(jnp.int32, shape, len(shape) - 1)


def half_turn(x):
    width = x.shape[1]
    near = pltpu.roll(x, HEAD_SIZE // 2, 1)
    far = pltpu.roll(x, width - HEAD_SIZE // 2, 1)
    return jnp.where(lane_iota(x.shape) % HEAD_SIZE < HEAD_SIZE // 2, far, near)


def widen(table, width):
    return jnp.concatenate([table] * (width // table.shape[1]), axis=1)


def put_masked(x, out):
    rows = x.shape[0]
    left = lane_iota((rows, PAIR)) < HEAD_SIZE
    for g in range(GROUPS):
        tile = x[:, g * PAIR : (g + 1) * PAIR]
        turned = pltpu.roll(tile, HEAD_SIZE, 1)
        if g % 2 == 0:
            pair = (jnp.where(left, tile, 0.0), jnp.where(left, turned, 0.0))
        else:
            pair = (jnp.where(left, 0.0, turned), jnp.where(left, 0.0, tile))
        for j in range(2):
            out[g, j * rows : (j + 1) * rows, :] = pair[j].astype(bf16)


def in_order(core, m, o):
    a = jnp.where(core == 0, m, o)
    b = jnp.where(core == 0, o, m)
    return jnp.concatenate([a[:CH], b[:CH], a[CH:], b[CH:]], axis=0)


def lanes_at(index, depth):
    return pl.ds(pl.multiple_of(index * depth, depth), depth)


def put_tile(sc, ref, per_shard, index, value):
    shard = (index // per_shard) ^ sc[2]
    row = shard * (per_shard * R) + (index % per_shard) * R
    ref[pl.ds(pl.multiple_of(row, R), R), :] = value.astype(ref.dtype)


def flag_base(n_seq):
    return 4 + 2 * n_seq


def qkv_kernel(
    sc, mine, other, cos, sin, w_own, w_rec_q, w_rec_kv, gain, a_t, b_q, b_k, b_v, g_qk, ones,
    u_out, raw_out, qm_out, kv_out, u_s, b_s,
):
    core = sc[0]
    a = jnp.where(core == 0, mine[0], other[0])
    b = jnp.where(core == 0, other[0], mine[0])
    x = jnp.concatenate([a, b], axis=0).astype(f32)
    inv = lax.rsqrt(jnp.mean(x * x, axis=1, keepdims=True) + epsilon)
    u = (x * inv * gain[...]).astype(bf16)
    u_s[...] = u
    u_out[...] = u
    depth = w_own.shape[0]

    @pl.when(pl.program_id(0) == 0)
    def _():
        b_s[...] = jnp.zeros_like(b_s)
        b_s[0:R, 0:QW] = b_q[0]
        b_s[R : 2 * R, QW : QW + KW] = b_k[0]
        b_s[2 * R : 3 * R, QW + KW : EW] = b_v[0]

    rank = mm_nt(u, a_t[0]).astype(bf16)
    raw = mm(u_s[:, lanes_at(core, depth)], w_own[...])
    u_rec = u_s[:, lanes_at(1 - core, depth)]
    raw += jnp.concatenate([mm(u_rec, w_rec_q[...]), mm(u_rec, w_rec_kv[...])], axis=1)
    raw += mm(rank, b_s[...])
    qk = raw[:, : QW + KW]
    raw_out[...] = qk
    normed = qk * lax.rsqrt(head_mean(qk * qk, ones[...]) + epsilon) * g_qk[...]
    turned = normed * widen(cos[...], QW + KW) + half_turn(normed) * widen(sin[...], QW + KW)

    put_masked(turned[:, :QW] * (1.0 / math.sqrt(HEAD_SIZE)), qm_out)
    kv_out[...] = jnp.concatenate([turned[:, QW:], raw[:, QW + KW :]], axis=1).astype(bf16)


def qkv_call(sc, mine, other, cos, sin, w_own, w_rec_q, w_rec_kv, gain, a_t, b_q, b_k, b_v, g_qk, ones):
    rows, width = mine.shape
    depth = w_own.shape[0]
    n = TOK // 2

    def rows_spec(cols):
        return pl.BlockSpec((n, cols), lambda i, s: (i, 0))

    half_spec = pl.BlockSpec((1, rows // 2, width), lambda i, s: (i, 0, 0))
    return pl.pallas_call(
        qkv_kernel,
        grid_spec=pltpu.PrefetchScalarGridSpec(
            num_scalar_prefetch=1,
            grid=(2,),
            in_specs=[
                half_spec, half_spec,
                rows_spec(PAIR), rows_spec(PAIR),
                whole((depth, EW)), whole((depth, QW)), whole((depth, 2 * KW)),
                whole((1, width)),
                pl.BlockSpec((1, 3 * R, width), lambda i, s: (s[1], 0, 0)),
                pl.BlockSpec((1, R, QW), lambda i, s: (s[1], 0, s[0])),
                pl.BlockSpec((1, R, KW), lambda i, s: (s[1], 0, s[0])),
                pl.BlockSpec((1, R, KW), lambda i, s: (s[1], 0, s[0])),
                whole((1, QW + KW)), whole(ones.shape),
            ],
            out_specs=[
                rows_spec(width), rows_spec(QW + KW),
                pl.BlockSpec((GROUPS, TOK, PAIR), lambda i, s: (0, i, 0)),
                rows_spec(2 * KW),
            ],
            scratch_shapes=[pltpu.VMEM((n, width), bf16), pltpu.VMEM((3 * R, EW), bf16)],
        ),
        out_shape=[
            jax.ShapeDtypeStruct((TOK, width), bf16),
            jax.ShapeDtypeStruct((TOK, QW + KW), f32),
            jax.ShapeDtypeStruct((GROUPS, 2 * TOK, PAIR), bf16),
            jax.ShapeDtypeStruct((TOK, 2 * KW), bf16),
        ],
        compiler_params=params(20),
        cost_estimate=cost(1e8, 1e6),
        name="qkv",
    )(
        sc, mine.reshape(2, rows // 2, width), other.reshape(2, rows // 2, width), cos, sin,
        w_own, w_rec_q, w_rec_kv, gain, a_t, b_q, b_k, b_v, g_qk, ones,
    )


def block_mask(sc, base, first, high, keys_first):
    shape = (2 * CH, 2 * CH)
    row = lax.broadcasted_iota(jnp.int32, shape, 0)
    col = lax.broadcasted_iota(jnp.int32, shape, 1)
    q, k = (col, row) if keys_first else (row, col)

    def pick(qb, kb):
        if first and qb == kb:
            return (k <= q).astype(f32)
        flag = sc[base + qb * 2 + kb]
        flag = 1 - flag if high else flag
        return flag.astype(f32)

    by_key = [jnp.where(k < CH, pick(qb, 0), pick(qb, 1)) for qb in range(2)]
    return jnp.where(q < CH, by_key[0], by_key[1])


def attend_kernel(bases, first, sc, qm, *rest):
    kvs = rest[: 2 * len(bases)]
    if first:
        acc_out, mask, vx = rest[2 * len(bases) :]
    else:
        acc_in, acc_out, mask, vx = rest[2 * len(bases) :]
    g = pl.program_id(0)
    n = 2 * CH

    @pl.when(g == 0)
    def _():
        for i, base in enumerate(bases):
            mask[i, 0] = block_mask(sc, base, first, False, False).astype(bf16)
            mask[i, 1] = block_mask(sc, base, first, True, False).astype(bf16)
        vx[:, :, PAIR:] = jnp.ones((len(bases), TOK, PAIR), bf16)

    o_low = o_high = None
    for i in range(len(bases)):
        k, v = kvs[2 * i], kvs[2 * i + 1]
        vx[i, :, :PAIR] = v[...]
        s_high = mm_nt(qm[0, 2 * n :, :], k[...])
        s_low = mm_nt(qm[0, : 2 * n, :], k[:n, :])
        p_all = jnp.exp(s_high[:, :n]).astype(bf16)
        p_high = jnp.exp(s_high[:, n:]).astype(bf16)
        p_low = jnp.exp(s_low).astype(bf16)
        m_low, m_high = mask[i, 0], mask[i, 1]
        p_high = jnp.concatenate([p_high[:n] * m_high, p_high[n:] * m_high], axis=0)
        p_low = jnp.concatenate([p_low[:n] * m_low, p_low[n:] * m_low], axis=0)
        high = mm(jnp.concatenate([p_all, p_high], axis=1), vx[i])
        low = mm(p_low, vx[i, :n, :])
        o_high = high if i == 0 else o_high + high
        o_low = low if i == 0 else o_low + low
    left = lane_iota((n, PAIR)) < HEAD_SIZE
    even = g % 2 == 0
    for lh, o in ((0, o_low), (1, o_high)):
        rows = slice(lh * n, (lh + 1) * n)
        o0, o1 = o[:n, :PAIR], o[n:, :PAIR]
        move = pltpu.roll(jnp.where(even, o1, o0), HEAD_SIZE, 1)
        value = jnp.where(left, jnp.where(even, o0, move), jnp.where(even, move, o1))
        norm = jnp.where(left, o[:n, PAIR:], o[n:, PAIR:])
        if not first:
            value += acc_in[0, rows, :PAIR]
            norm += acc_in[0, rows, PAIR:]
        acc_out[0, rows, :PAIR] = value
        acc_out[0, rows, PAIR:] = norm


def attend_call(bases, sc, qm, kvs, acc):
    first = acc is None
    acc_spec = pl.BlockSpec((1, TOK, 2 * PAIR), lambda g, s: (g, 0, 0))
    kv_specs = [
        pl.BlockSpec((TOK, PAIR), lambda g, s: (0, g // 2)),
        pl.BlockSpec((TOK, PAIR), lambda g, s: (0, GROUPS // 2 + g // 2)),
    ]
    n = len(bases)
    return pl.pallas_call(
        functools.partial(attend_kernel, bases, first),
        grid_spec=pltpu.PrefetchScalarGridSpec(
            num_scalar_prefetch=1,
            grid=(GROUPS,),
            in_specs=[pl.BlockSpec((1, 2 * TOK, PAIR), lambda g, s: (g, 0, 0))]
            + kv_specs * n
            + ([] if first else [acc_spec]),
            out_specs=acc_spec,
            scratch_shapes=[
                pltpu.VMEM((n, 2, 2 * CH, 2 * CH), bf16),
                pltpu.VMEM((n, TOK, 2 * PAIR), bf16),
            ],
        ),
        out_shape=jax.ShapeDtypeStruct((GROUPS, TOK, 2 * PAIR), f32),
        input_output_aliases={} if first else {2 + 2 * n: 0},
        compiler_params=params(12 if n < 8 else 40),
        cost_estimate=cost(1e8, 1e6),
        name="attend",
    )(sc, qm, *[kv for kv in kvs for _ in range(2)], *([] if first else [acc]))


def head_lines(tiles, out):
    rows = tiles[0].shape[0]
    lane = lane_iota(tiles[0].shape) % HEAD_SIZE
    packed = tiles[0]
    for g in range(1, GROUPS):
        packed = jnp.where(lane == g, tiles[g], packed)
    turned = packed.T
    for g in range(GROUPS):
        for j in range(2):
            row = j * HEAD_SIZE + g
            out[g, :, j * rows : (j + 1) * rows] = turned[row : row + 1, :]


def project_kernel(sc, acc, w_o, a_o, b_o, ob_out, mix_out, lse_out):
    parts, norms = [], []
    for g in range(GROUPS):
        norm = acc[g, :, PAIR:]
        parts.append(acc[g, :, :PAIR] / norm)
        norms.append(norm)
    ob = jnp.concatenate(parts, axis=1).astype(bf16)
    ob_out[...] = ob
    head_lines(norms, lse_out)
    lse_out[...] = jnp.log(lse_out[...])
    rank = mm_nt(ob, a_o[0]).astype(bf16)
    mix_out[...] = (mm(ob, w_o[...]) + mm(rank, b_o[0])).astype(bf16)


def project_call(sc, acc, w_o, a_o, b_o):
    width = w_o.shape[1]
    n = TOK // 2
    return pl.pallas_call(
        project_kernel,
        grid_spec=pltpu.PrefetchScalarGridSpec(
            num_scalar_prefetch=1,
            grid=(2,),
            in_specs=[
                pl.BlockSpec((GROUPS, n, 2 * PAIR), lambda i, s: (0, i, 0)),
                whole(w_o.shape),
                pl.BlockSpec((1, R, QW), lambda i, s: (s[1], 0, s[0])),
                pl.BlockSpec((1, R, width), lambda i, s: (s[1], 0, 0)),
            ],
            out_specs=[
                pl.BlockSpec((n, QW), lambda i, s: (i, 0)),
                pl.BlockSpec((n, width), lambda i, s: (i, 0)),
                pl.BlockSpec((GROUPS, 1, 2 * n), lambda i, s: (0, 0, i)),
            ],
        ),
        out_shape=[
            jax.ShapeDtypeStruct((TOK, QW), bf16),
            jax.ShapeDtypeStruct((TOK, width), bf16),
            jax.ShapeDtypeStruct((GROUPS, 1, 2 * TOK), f32),
        ],
        compiler_params=params(14),
        cost_estimate=cost(1e8, 1e6),
        name="project",
    )(sc, acc, w_o, a_o, b_o)


def hidden_back_kernel(sc, c_mine, c_low, c_high, w_d, a_d, b_d, out, ed_out, drT_out, ed_s, dr_s):
    @pl.when(pl.program_id(0) == 0)
    def _():
        c_other = jnp.concatenate([c_low[...], c_high[...]], axis=0)
        ed = in_order(sc[0], c_mine[...], c_other)
        ed_s[...] = ed
        ed_out[...] = ed
        dr_s[...] = mm_nt(ed, b_d[0]).astype(bf16)
        drT_out[...] = mm_nt(b_d[0], ed).astype(bf16)

    out[...] = mm_nt(ed_s[...], w_d[...]) + mm(dr_s[...], a_d[0])


def hidden_back_call(sc, c_mine, c_low, c_high, w_d, a_d, b_d):
    rows, width = c_mine.shape
    return pl.pallas_call(
        hidden_back_kernel,
        grid_spec=pltpu.PrefetchScalarGridSpec(
            num_scalar_prefetch=1,
            grid=(NT,),
            in_specs=[
                whole((rows, width)), whole((CH, width)), whole((CH, width)),
                pl.BlockSpec((TF, width), lambda i, s: (i, 0)),
                pl.BlockSpec((1, R, TF), lambda i, s: (s[1], 0, s[0] * NT + i)),
                pl.BlockSpec((1, R, width), lambda i, s: (s[1], 0, 0)),
            ],
            out_specs=[
                pl.BlockSpec((TOK, TF), lambda i, s: (0, i)), whole((TOK, width)), whole((R, TOK)),
            ],
            scratch_shapes=[pltpu.VMEM((TOK, width), bf16), pltpu.VMEM((TOK, R), bf16)],
        ),
        out_shape=[
            jax.ShapeDtypeStruct((TOK, HF), f32),
            jax.ShapeDtypeStruct((TOK, width), bf16),
            jax.ShapeDtypeStruct((R, TOK), bf16),
        ],
        compiler_params=params(20),
        cost_estimate=cost(1e8, 1e6),
        name="hidden_back",
    )(sc, c_mine, c_low, c_high, w_d, a_d, b_d)


GU_TILES = 3 * HF // 128


def early_tiles(width):
    return GU_TILES + 4 * width // 128 + QW // 128


def ffn_kernel(
    per_shard,
    sc, mine, other, mix_a, mix_b, dh_tile, ed, drdT, gain, wg_own, wu_own, wg_rec, wu_rec, w_d,
    a_gu, b_gu, a_d, b_d,
    y_out, down_out, du_out, pay,
    u_s, down_s, du_s, rgu_s, rguT_s, rdT_s, drguT_s,
):
    i = pl.program_id(0)
    core = sc[0]
    depth = wg_own.shape[0]
    width = u_s.shape[1]
    own = lanes_at(core, depth)
    rec = lanes_at(1 - core, depth)

    @pl.when(i == 0)
    def _():
        x = in_order(core, mine[...], other[...]).astype(f32)
        h = x + (mix_a[...].astype(f32) + mix_b[...].astype(f32))
        inv = lax.rsqrt(jnp.mean(h * h, axis=1, keepdims=True) + epsilon)
        u = (h * inv * gain[...]).astype(bf16)
        u_s[...] = u
        rgu_s[...] = mm_nt(u, a_gu[0]).astype(bf16)
        rguT_s[...] = mm_nt(a_gu[0], u).astype(bf16)
        rdT_s[...] = jnp.zeros_like(rdT_s)
        drguT_s[...] = jnp.zeros_like(drguT_s)
        pay[...] = jnp.zeros_like(pay)

    u_own, u_rec = u_s[:, own], u_s[:, rec]
    gate = mm(u_own, wg_own[...]) + mm(u_rec, wg_rec[...]) + mm(rgu_s[:, :R], b_gu[0, 0])
    up = mm(u_own, wu_own[...]) + mm(u_rec, wu_rec[...]) + mm(rgu_s[:, R:], b_gu[0, 1])
    d_hid = dh_tile[...]
    sig = jax.nn.sigmoid(gate)
    silu = gate * sig
    hid = (silu * up).astype(bf16)
    e_g = (d_hid * up * (sig * (1.0 + gate * (1.0 - sig)))).astype(bf16)
    e_u = (d_hid * silu).astype(bf16)
    down = mm(hid, w_d[...])
    du_own = mm_nt(e_g, wg_own[...]) + mm_nt(e_u, wu_own[...])
    du_rec = mm_nt(e_g, wg_rec[...]) + mm_nt(e_u, wu_rec[...])

    @pl.when(i == 0)
    def _():
        down_s[...] = down
        du_s[:, own] = du_own
        du_s[:, rec] = du_rec

    @pl.when(i > 0)
    def _():
        down_s[...] += down
        du_s[:, own] += du_own
        du_s[:, rec] += du_rec

    rdT_s[...] += mm_nt(a_d[0], hid)
    drguT_s[:R, :] += mm_nt(b_gu[0, 0], e_g)
    drguT_s[R:, :] += mm_nt(b_gu[0, 1], e_u)
    grads = (mm(rguT_s[:R], e_g), mm(rguT_s[R:], e_u), mm(drdT[...], hid))
    for t in range(TF // 128):
        for q in range(3):
            index = (i * (TF // 128) + t) * 3 + q
            put_tile(sc, pay, per_shard, index, grads[q][:, t * 128 : (t + 1) * 128])

    @pl.when(i == pl.num_programs(0) - 1)
    def _():
        rdT = rdT_s[...].astype(bf16)
        drT = drguT_s[...].astype(bf16)
        tn = (((0,), (0,)), ((), ()))
        down_s[...] += lax.dot_general(rdT, b_d[0], tn, preferred_element_type=f32)
        du_out[...] = (
            du_s[...] + lax.dot_general(drT, a_gu[0], tn, preferred_element_type=f32)
        ).astype(bf16)
        for lh in range(2):
            at = slice(lh * CH, (lh + 1) * CH)
            row = pl.ds(pl.multiple_of(lh * 2 * CH + core * CH, CH), CH)
            out = pl.ds(pl.multiple_of(lh * 2 * CH + (1 - core) * CH, CH), CH)
            mix = mix_a[row, :].astype(f32) + mix_b[row, :].astype(f32)
            y_out[at, :] = (mine[at, :].astype(f32) + mix) + down_s[row, :]
            down_out[at, :] = down_s[out, :].astype(bf16)
        gb = mm(rdT, ed[...])
        ga = mm(drT, u_s[...])
        for t in range(width // 128):
            at = slice(t * 128, (t + 1) * 128)
            put_tile(sc, pay, per_shard, GU_TILES + t, gb[:, at])
            for q in range(2):
                index = GU_TILES + width // 128 + t * 2 + q
                put_tile(sc, pay, per_shard, index, ga[q * R : (q + 1) * R, at])


def ffn_call(
    half, sc, mine, other, mix_a, mix_b, d_hid, ed, drdT, gain, w_gu, w_rec, w_d, a_gu, b_gu,
    a_d, b_d,
):
    rows, width = mine.shape
    depth = w_gu.shape[0]
    per_shard = -(-early_tiles(width) // half)
    block = whole((rows, width))
    full = whole((TOK, width))
    return pl.pallas_call(
        functools.partial(ffn_kernel, per_shard),
        grid_spec=pltpu.PrefetchScalarGridSpec(
            num_scalar_prefetch=1,
            grid=(NT,),
            in_specs=[
                block, block, full, full,
                pl.BlockSpec((TOK, TF), lambda i, s: (0, i)),
                full, whole((R, TOK)), whole((1, width)),
                pl.BlockSpec((depth, TF), lambda i, s: (0, s[0] * NT + i)),
                pl.BlockSpec((depth, TF), lambda i, s: (0, 2 * NT + s[0] * NT + i)),
                pl.BlockSpec((depth, TF), lambda i, s: (0, i)),
                pl.BlockSpec((depth, TF), lambda i, s: (0, NT + i)),
                pl.BlockSpec((TF, width), lambda i, s: (i, 0)),
                pl.BlockSpec((1, 2 * R, width), lambda i, s: (s[1], 0, 0)),
                pl.BlockSpec((1, 2, R, TF), lambda i, s: (s[1], 0, 0, s[0] * NT + i)),
                pl.BlockSpec((1, R, TF), lambda i, s: (s[1], 0, s[0] * NT + i)),
                pl.BlockSpec((1, R, width), lambda i, s: (s[1], 0, 0)),
            ],
            out_specs=[block, block, full, whole((half * per_shard * R, 128))],
            scratch_shapes=[
                pltpu.VMEM((TOK, width), bf16),
                pltpu.VMEM((TOK, width), f32),
                pltpu.VMEM((TOK, width), f32),
                pltpu.VMEM((TOK, 2 * R), bf16),
                pltpu.VMEM((2 * R, TOK), bf16),
                pltpu.VMEM((R, TOK), f32),
                pltpu.VMEM((2 * R, TOK), f32),
            ],
        ),
        out_shape=[
            jax.ShapeDtypeStruct((rows, width), f32),
            jax.ShapeDtypeStruct((rows, width), bf16),
            jax.ShapeDtypeStruct((TOK, width), bf16),
            jax.ShapeDtypeStruct((half * per_shard * R, 128), bf16),
        ],
        compiler_params=params(40),
        cost_estimate=cost(1e9, 2.5e6),
        name="ffn",
    )(
        sc, mine, other, mix_a, mix_b, d_hid, ed, drdT, gain, w_gu, w_gu, w_rec, w_rec, w_d,
        a_gu, b_gu, a_d, b_d,
    )


def back_mix_kernel(
    per_shard,
    sc, mine, other, mix_a, mix_b, ed, du_a, du_b, gain, w_o, a_o, b_o, ob, ones, pay_in,
    dh_out, dom_out, delta_out, pay, dh_s, gb_s, ga_s,
):
    i = pl.program_id(0)
    core = sc[0]

    def pair(m, o):
        a = jnp.where(core == 0, m[0], o[0])
        b = jnp.where(core == 0, o[0], m[0])
        return jnp.concatenate([a, b], axis=0).astype(f32)

    hv = pair(mine, other) + (mix_a[...].astype(f32) + mix_b[...].astype(f32))
    inv = lax.rsqrt(jnp.mean(hv * hv, axis=1, keepdims=True) + epsilon)
    w = gain[...] * (du_a[...].astype(f32) + du_b[...].astype(f32))
    dh = ed[...].astype(f32) + inv * w - hv * (
        inv * inv * inv * jnp.mean(hv * w, axis=1, keepdims=True)
    )
    dh_s[...] = dh
    dh_out[...] = dh_s[pl.ds(pl.multiple_of(core * CH, CH), CH), :]
    e_o = dh.astype(bf16)
    obv = ob[...]
    dr = mm_nt(e_o, b_o[0]).astype(bf16)
    drT = mm_nt(b_o[0], e_o).astype(bf16)
    rT = mm_nt(a_o[0], obv).astype(bf16)
    gb = mm(rT, e_o)
    ga = mm(drT, obv)

    @pl.when(i == 0)
    def _():
        gb_s[...] = gb
        ga_s[...] = ga

    @pl.when(i > 0)
    def _():
        gb_s[...] += gb
        ga_s[...] += ga
        pay[...] = pay_in[...]
        n_w = dh_s.shape[1] // 128
        for t in range(n_w):
            index = GU_TILES + 3 * n_w + t
            put_tile(sc, pay, per_shard, index, gb_s[:, t * 128 : (t + 1) * 128])
        for t in range(QW // 128):
            index = GU_TILES + 4 * n_w + t
            put_tile(sc, pay, per_shard, index, ga_s[:, t * 128 : (t + 1) * 128])

    d_o = (mm_nt(e_o, w_o[...]) + mm(dr, a_o[0])).astype(bf16).astype(f32)
    prod = head_mean(d_o * obv.astype(f32), ones[...]) * HEAD_SIZE
    head_lines([prod[:, g * PAIR : (g + 1) * PAIR] for g in range(GROUPS)], delta_out)
    put_masked(d_o, dom_out)


def back_mix_call(
    half, sc, mine, other, mix_a, mix_b, ed, du_a, du_b, gain, w_o, a_o, b_o, ob, ones, pay,
):
    rows, width = mine.shape
    per_shard = -(-early_tiles(width) // half)
    n = TOK // 2
    block = pl.BlockSpec((1, rows // 2, width), lambda i, s: (i, 0, 0))
    full = pl.BlockSpec((n, width), lambda i, s: (i, 0))

    def two(v):
        return v.reshape(2, rows // 2, width)

    return pl.pallas_call(
        functools.partial(back_mix_kernel, per_shard),
        grid_spec=pltpu.PrefetchScalarGridSpec(
            num_scalar_prefetch=1,
            grid=(2,),
            in_specs=[
                block, block, full, full, full, full, full,
                whole((1, width)), whole(w_o.shape),
                pl.BlockSpec((1, R, QW), lambda i, s: (s[1], 0, s[0])),
                pl.BlockSpec((1, R, width), lambda i, s: (s[1], 0, 0)),
                pl.BlockSpec((n, QW), lambda i, s: (i, 0)),
                whole(ones.shape), whole(pay.shape),
            ],
            out_specs=[
                pl.BlockSpec((rows // 2, width), lambda i, s: (i, 0)),
                pl.BlockSpec((GROUPS, TOK, PAIR), lambda i, s: (0, i, 0)),
                pl.BlockSpec((GROUPS, 1, 2 * n), lambda i, s: (0, 0, i)),
                whole(pay.shape),
            ],
            scratch_shapes=[
                pltpu.VMEM((n, width), f32), pltpu.VMEM((R, width), f32), pltpu.VMEM((R, QW), f32),
            ],
        ),
        out_shape=[
            jax.ShapeDtypeStruct((rows, width), f32),
            jax.ShapeDtypeStruct((GROUPS, 2 * TOK, PAIR), bf16),
            jax.ShapeDtypeStruct((GROUPS, 1, 2 * TOK), f32),
            jax.ShapeDtypeStruct(pay.shape, pay.dtype),
        ],
        input_output_aliases={14: 3},
        compiler_params=params(24),
        cost_estimate=cost(1e8, 1e6),
        name="back_mix",
    )(
        sc, two(mine), two(other), mix_a, mix_b, ed, du_a, du_b, gain,
        w_o, a_o, b_o, ob, ones, pay,
    )


def attend_back_kernel(base, first, has_dq, sc, qm, dom, k, v, lse, delta, *rest):
    if has_dq:
        dq_in, dq_out, dkv_out, dkv, kt, mask = rest
    else:
        dq_out, dkv_out, dkv, kt, mask = rest
    g = pl.program_id(0)
    side = g % 2
    n = 2 * CH

    @pl.when(g == 0)
    def _():
        mask[0] = block_mask(sc, base, first, False, True)
        mask[1] = block_mask(sc, base, first, True, True)

    @pl.when(side == 0)
    def _():
        kt[...] = k[...].astype(f32).T.astype(bf16)

    kth = kt.at[pl.ds(pl.multiple_of(side * HEAD_SIZE, HEAD_SIZE), HEAD_SIZE), :]
    q_all, do_all = qm[0], dom[0]
    q_high, do_high = qm[0, 2 * n :, :], dom[0, 2 * n :, :]
    s_low = mm_nt(k[:n, :], q_all)
    s_high = mm_nt(k[n:, :], q_high)
    dp_low = mm_nt(v[:n, :], do_all)
    dp_high = mm_nt(v[n:, :], do_high)
    m_low, m_high = mask[0], mask[1]
    lse_all, delta_all = lse[0], delta[0]
    p_low = jnp.exp(s_low - lse_all)
    p_low = jnp.concatenate(
        [p_low[:, :n] * m_low, p_low[:, n : 2 * n] * m_low, p_low[:, 2 * n :]], axis=1
    )
    p_high = jnp.exp(s_high - lse_all[:, 2 * n :])
    p_high = jnp.concatenate([p_high[:, :n] * m_high, p_high[:, n:] * m_high], axis=1)
    ds_low = (p_low * (dp_low - delta_all)).astype(bf16)
    ds_high = (p_high * (dp_high - delta_all[:, 2 * n :])).astype(bf16)
    p_low, p_high = p_low.astype(bf16), p_high.astype(bf16)
    dk_low, dk_high = mm(ds_low, q_all), mm(ds_high, q_high)
    dv_low, dv_high = mm(p_low, do_all), mm(p_high, do_high)
    dq_low = mm(kth[:, :n], ds_low)
    dq_high = mm(kth[:, n:], ds_high)
    dq = jnp.concatenate([dq_low[:, : 2 * n], dq_low[:, 2 * n :] + dq_high], axis=1)
    dq_out[0] = dq_in[0] + dq if has_dq else dq

    @pl.when(side == 0)
    def _():
        dkv[0, :n, :] = dk_low
        dkv[0, n:, :] = dk_high
        dkv[1, :n, :] = dv_low
        dkv[1, n:, :] = dv_high

    @pl.when(side == 1)
    def _():
        dkv_out[0, :n, :] = (dkv[0, :n, :] + dk_low).astype(dkv_out.dtype)
        dkv_out[0, n:, :] = (dkv[0, n:, :] + dk_high).astype(dkv_out.dtype)
        dkv_out[1, :n, :] = (dkv[1, :n, :] + dv_low).astype(dkv_out.dtype)
        dkv_out[1, n:, :] = (dkv[1, n:, :] + dv_high).astype(dkv_out.dtype)


def attend_back_call(base, first, sc, qm, dom, kv, lse, delta, dq):
    has_dq = dq is not None
    dq_spec = pl.BlockSpec((1, HEAD_SIZE, 2 * TOK), lambda g, s: (g, 0, 0))
    row_spec = pl.BlockSpec((1, 1, 2 * TOK), lambda g, s: (g, 0, 0))
    return pl.pallas_call(
        functools.partial(attend_back_kernel, base, first, has_dq),
        grid_spec=pltpu.PrefetchScalarGridSpec(
            num_scalar_prefetch=1,
            grid=(GROUPS,),
            in_specs=[
                pl.BlockSpec((1, 2 * TOK, PAIR), lambda g, s: (g, 0, 0)),
                pl.BlockSpec((1, 2 * TOK, PAIR), lambda g, s: (g, 0, 0)),
                pl.BlockSpec((TOK, PAIR), lambda g, s: (0, g // 2)),
                pl.BlockSpec((TOK, PAIR), lambda g, s: (0, GROUPS // 2 + g // 2)),
                row_spec, row_spec,
            ]
            + ([dq_spec] if has_dq else []),
            out_specs=[dq_spec, pl.BlockSpec((2, TOK, PAIR), lambda g, s: (0, 0, g // 2))],
            scratch_shapes=[
                pltpu.VMEM((2, TOK, PAIR), f32),
                pltpu.VMEM((PAIR, TOK), bf16),
                pltpu.VMEM((2, 2 * CH, 2 * CH), f32),
            ],
        ),
        out_shape=[
            jax.ShapeDtypeStruct((GROUPS, HEAD_SIZE, 2 * TOK), f32),
            jax.ShapeDtypeStruct((2, TOK, KW), f32 if first else bf16),
        ],
        input_output_aliases={7: 0} if has_dq else {},
        compiler_params=params(16),
        cost_estimate=cost(1e8, 1e6),
        name="attend_back",
    )(sc, qm, dom, kv, kv, lse, delta, *([dq] if has_dq else []))


def late_tiles(width):
    return 4 * width // 128


def qkv_back_kernel(per_shard, parts, sc, dq, dkv, *rest):
    got = rest[:parts]
    (raw, cos, sin, g_qk, ones, u, w_own, w_rec_q, w_rec_kv, a_t, b_q, b_k, b_v,
     du_out, send_out, pay, e_s, b_s, du_s, ga_s, gb_s) = rest[parts:]
    i = pl.program_id(0)
    core = sc[0]
    width = QW + KW

    @pl.when(i == 0)
    def _():
        b_s[...] = jnp.zeros_like(b_s)
        b_s[0:R, 0:QW] = b_q[0]
        b_s[R : 2 * R, QW:width] = b_k[0]
        b_s[2 * R : 3 * R, width:EW] = b_v[0]
        ga_s[...] = jnp.zeros_like(ga_s)
        gb_s[...] = jnp.zeros_like(gb_s)
        pay[...] = jnp.zeros_like(pay)

    m = dq.shape[2] // 2
    heads = [dq[g, :, j * m : (j + 1) * m] for g in range(GROUPS) for j in range(2)]
    d_q = jnp.concatenate(heads, axis=0).T * (1.0 / math.sqrt(HEAD_SIZE))
    d_k, d_v = dkv[0], dkv[1]
    for n in range(parts):
        d_k = d_k + got[n][0].astype(f32)
        d_v = d_v + got[n][1].astype(f32)
    grad = jnp.concatenate([d_q, d_k], axis=1)
    grad = grad * widen(cos[...], width) - half_turn(grad) * widen(sin[...], width)
    v = raw[...]
    inv = lax.rsqrt(head_mean(v * v, ones[...]) + epsilon)
    w = grad * g_qk[...]
    grad = inv * w - v * (inv * inv * inv) * head_mean(v * w, ones[...])
    e_s[:, :width] = grad.astype(bf16)
    e_s[:, width:] = d_v.astype(bf16)
    e = e_s[...]
    uv = u[...]
    dr = mm_nt(e, b_s[...]).astype(bf16)
    drT = mm_nt(b_s[...], e).astype(bf16)
    rT = mm_nt(a_t[0], uv).astype(bf16)
    gb_s[...] += mm(rT, e)
    ga_s[...] += mm(drT, uv)
    depth = w_own.shape[0]
    du_s[...] = mm(dr, a_t[0])
    du_s[:, lanes_at(core, depth)] += mm_nt(e, w_own[...])
    du_s[:, lanes_at(1 - core, depth)] += mm_nt(e[:, :QW], w_rec_q[...]) + mm_nt(
        e[:, QW:], w_rec_kv[...]
    )
    du_out[...] = du_s[pl.ds(pl.multiple_of(core * CH, CH), CH), :]
    send_out[...] = du_s[pl.ds(pl.multiple_of((1 - core) * CH, CH), CH), :].astype(bf16)

    @pl.when(i == pl.num_programs(0) - 1)
    def _():
        n = uv.shape[1] // 128
        for t in range(n):
            at = slice(t * 128, (t + 1) * 128)
            for q in range(3):
                put_tile(sc, pay, per_shard, t * 3 + q, ga_s[q * R : (q + 1) * R, at])
        for t in range(EW // 128):
            at = slice(t * 128, (t + 1) * 128)
            q = 0 if t < QW // 128 else (1 if t < width // 128 else 2)
            put_tile(sc, pay, per_shard, 3 * n + t, gb_s[q * R : (q + 1) * R, at])


def qkv_back_call(
    half, sc, dq, dkv, got, raw, cos, sin, g_qk, ones, u, w_own, w_rec_q, w_rec_kv, a_t, b_q, b_k,
    b_v,
):
    width = u.shape[1]
    depth = w_own.shape[0]
    parts = len(got)
    n = TOK // 2
    per_shard = -(-late_tiles(width) // half)

    def rows_spec(cols):
        return pl.BlockSpec((n, cols), lambda i, s: (i, 0))

    dkv_spec = pl.BlockSpec((2, n, KW), lambda i, s: (0, i, 0))
    half_spec = pl.BlockSpec((CH, width), lambda i, s: (i, 0))
    return pl.pallas_call(
        functools.partial(qkv_back_kernel, per_shard, parts),
        grid_spec=pltpu.PrefetchScalarGridSpec(
            num_scalar_prefetch=1,
            grid=(2,),
            in_specs=[pl.BlockSpec((GROUPS, HEAD_SIZE, 2 * n), lambda i, s: (0, 0, i)), dkv_spec]
            + [dkv_spec] * parts
            + [
                rows_spec(QW + KW), rows_spec(PAIR), rows_spec(PAIR), whole(g_qk.shape),
                whole(ones.shape), rows_spec(width), whole(w_own.shape),
                whole(w_rec_q.shape), whole(w_rec_kv.shape),
                pl.BlockSpec((1, 3 * R, width), lambda i, s: (s[1], 0, 0)),
                pl.BlockSpec((1, R, QW), lambda i, s: (s[1], 0, s[0])),
                pl.BlockSpec((1, R, KW), lambda i, s: (s[1], 0, s[0])),
                pl.BlockSpec((1, R, KW), lambda i, s: (s[1], 0, s[0])),
            ],
            out_specs=[half_spec, half_spec, whole((half * per_shard * R, 128))],
            scratch_shapes=[
                pltpu.VMEM((n, EW), bf16), pltpu.VMEM((3 * R, EW), bf16),
                pltpu.VMEM((n, width), f32), pltpu.VMEM((3 * R, width), f32),
                pltpu.VMEM((3 * R, EW), f32),
            ],
        ),
        out_shape=[
            jax.ShapeDtypeStruct((TOK // 2, width), f32),
            jax.ShapeDtypeStruct((TOK // 2, width), bf16),
            jax.ShapeDtypeStruct((half * per_shard * R, 128), bf16),
        ],
        compiler_params=params(24),
        cost_estimate=cost(1e8, 1e6),
        name="qkv_back",
    )(
        sc, dq, dkv, *got, raw, cos, sin, g_qk, ones, u, w_own, w_rec_q, w_rec_kv, a_t, b_q, b_k,
        b_v,
    )


def norm_back_kernel(x, du, got, dh, gain, out, low_out):
    v = x[...].astype(f32)
    inv = lax.rsqrt(jnp.mean(v * v, axis=1, keepdims=True) + epsilon)
    w = (du[...] + got[...].astype(f32)) * gain[...]
    grad = dh[...] + inv * w - v * (inv * inv * inv * jnp.mean(v * w, axis=1, keepdims=True))
    out[...] = grad
    low_out[...] = grad.astype(bf16)


def norm_back_call(x, du, got, dh, gain):
    rows, width = x.shape
    spec = pl.BlockSpec((rows // 2, width), lambda i: (i, 0))
    return pl.pallas_call(
        norm_back_kernel,
        grid=(2,),
        in_specs=[spec, spec, spec, spec, pl.BlockSpec((1, width), lambda i: (0, 0))],
        out_specs=[spec, spec],
        out_shape=[
            jax.ShapeDtypeStruct((rows, width), f32),
            jax.ShapeDtypeStruct((rows, width), bf16),
        ],
        compiler_params=params(10),
        cost_estimate=cost(1e7, 1e6),
        name="norm_back",
    )(x, du, got, dh, gain)


def home_kernel(stays, own, back, out):
    v = jnp.where(stays[0] == 1, own[...], back[...].astype(f32))
    n = v.shape[1] // 128
    for t in range(n):
        out[pl.ds(t, v.shape[0], stride=n), :] = v[:, t * 128 : (t + 1) * 128]


def home_call(stays, own, back):
    rows, width = own.shape
    n = width // 128
    spec = pl.BlockSpec((rows // 2, width), lambda i, s: (i, 0))
    out = pl.pallas_call(
        home_kernel,
        grid_spec=pltpu.PrefetchScalarGridSpec(
            num_scalar_prefetch=1,
            grid=(2,),
            in_specs=[spec, spec],
            out_specs=pl.BlockSpec((rows // 2 * n, 128), lambda i, s: (i, 0)),
        ),
        out_shape=jax.ShapeDtypeStruct((rows * n, 128), f32),
        compiler_params=params(8),
        cost_estimate=cost(1e7, 1e6),
        name="home",
    )(stays, own, back)
    return out.reshape(rows, 1, width)


def place_kernel(pieces, half, n_seq, per_shard, sc, own_core, twin, *rest):
    outs, box, sem = rest[:-2], rest[-2], rest[-1]
    core, place, own = sc[0], sc[2], sc[3]
    which = pl.program_id(0)
    parts, _, group = own_core.shape[:3]

    @pl.when(which == 0)
    def _():
        copies = []
        for c, source in enumerate((own_core, twin)):
            for part in range(parts):
                for k in range(half):
                    copies.append(
                        pltpu.make_async_copy(
                            source.at[part, k],
                            box.at[core ^ c, place ^ k, pl.ds(part * group, group)],
                            sem.at[(c * parts + part) * half + k],
                        )
                    )
        for copy in copies:
            copy.start()
        for copy in copies:
            copy.wait()

    for out in outs:
        out[...] = jnp.zeros_like(out)
    for b in range(2 * n_seq):
        rel = own ^ b

        @pl.when(sc[4 + b] == which)
        def _():
            for c in range(2):
                for index, target, lead, lane, shift in pieces:
                    at = lane + c * shift
                    rows = slice((index % per_shard) * R, (index % per_shard + 1) * R)
                    value = box[c, index // per_shard, rel, rows, :].astype(f32)
                    outs[target][(0,) + lead + (slice(at, at + 128),)] += value


def place_call(pieces, shapes, n_seq, sc, own_core, twin):
    parts, half, _, rows, _ = own_core.shape

    def out_spec(shape):
        zeros = (0,) * len(shape)
        return pl.BlockSpec((1,) + shape, lambda i, s: (i,) + zeros)

    return pl.pallas_call(
        functools.partial(place_kernel, pieces, half, n_seq, rows // R),
        grid_spec=pltpu.PrefetchScalarGridSpec(
            num_scalar_prefetch=1,
            grid=(ADAPTER_SETS,),
            in_specs=[pl.BlockSpec(memory_space=pl.ANY)] * 2,
            out_specs=[out_spec(shape) for shape in shapes],
            scratch_shapes=[
                pltpu.VMEM((2, half, 2 * n_seq, rows, 128), bf16),
                pltpu.SemaphoreType.DMA((2 * parts * half,)),
            ],
        ),
        out_shape=[jax.ShapeDtypeStruct((ADAPTER_SETS,) + shape, f32) for shape in shapes],
        compiler_params=params(24),
        cost_estimate=cost(1e7, 1e6),
        name="place",
    )(sc, own_core, twin)


def rope_parts():
    freq = np.exp(-math.log(rope_base) * 2.0 * np.arange(HEAD_SIZE // 2) / HEAD_SIZE)
    angle = np.arange(CH)[:, None] * freq[None, :]
    return freq, np.cos(angle).astype(np.float32), np.sin(angle).astype(np.float32)


def rope_tables(stretches):
    freq, cos_t, sin_t = rope_parts()
    angle = (stretches.astype(f32) * CH)[:, None] * jnp.asarray(freq.astype(np.float32))[None, :]
    cos_a, sin_a = jnp.cos(angle)[:, None, :], jnp.sin(angle)[:, None, :]
    cos = cos_a * cos_t[None] - sin_a * sin_t[None]
    sin = sin_a * cos_t[None] + cos_a * sin_t[None]
    return (
        jnp.concatenate([cos, cos, cos, cos], axis=-1).reshape(TOK, PAIR),
        jnp.concatenate([-sin, sin, -sin, sin], axis=-1).reshape(TOK, PAIR),
    )


def after(value, *earlier):
    return lax.optimization_barrier((value,) + earlier)[0]


def per_device(
    hidden_in, cotangent, query_key_value_weight, w_o, w_gu, w_down, g_attn, g_ffn, g_q,
    key_norm_gain, a_qkv, b_q, key_up_weight, value_up_weight, a_o, b_o, a_gu, b_gu, a_down,
    b_down, set_index, stretch_order,
):
    rows, _, width = hidden_in.shape
    n_ctx = lax.axis_size("ctx")
    n_seq = lax.axis_size("seq")
    half = n_ctx // 2
    core = lax.axis_index("wsh")
    ctx = lax.axis_index("ctx")
    side = ctx // half
    place = ctx % half
    own_seq = lax.axis_index("seq") * 2 + side
    stays = core == side

    def line(s, p, c):
        return (s * half + p) * 2 + c

    swap_pairs = [
        (line(s, p, c), line(c, p, s))
        for s in range(2) for p in range(half) for c in range(2) if s != c
    ]

    def swap(v):
        return lax.ppermute(v, ("ctx", "wsh"), swap_pairs)

    def other_core(v):
        return lax.ppermute(v, "wsh", [(0, 1), (1, 0)])

    def partner(v, k):
        return lax.ppermute(
            v, "ctx", [(s * half + p, s * half + (p ^ k)) for s in range(2) for p in range(half)]
        )

    def other_seq(v, d):
        pairs = [
            (s * n_ctx + i, (s ^ (d // 2)) * n_ctx + (i + half * (d % 2)) % n_ctx)
            for s in range(n_seq) for i in range(n_ctx)
        ]
        return lax.ppermute(v, ("seq", "ctx"), pairs)

    hid = hidden_in.reshape(rows, width)
    cot = cotangent.reshape(rows, width)
    mine = jnp.where(stays, hid, swap(hid))
    order = jnp.where(stays, stretch_order[0], swap(stretch_order)[0])
    other = other_core(mine)

    query_key_value_weight = after(query_key_value_weight, order)

    def cols(w, start, size, which):
        return lax.dynamic_slice_in_dim(w, start + which * size, size, 1)

    def qkv_cols(which):
        return jnp.concatenate(
            [
                cols(query_key_value_weight, 0, QW, which),
                cols(query_key_value_weight, 2 * QW, KW, which),
                cols(query_key_value_weight, 2 * QW + 2 * KW, KW, which),
            ],
            axis=1,
        )

    w_own = qkv_cols(core)
    w_send = after(qkv_cols(1 - core), mine)
    w_rec_q, w_rec_kv = other_core(w_send[:, :QW]), other_core(w_send[:, QW:])

    own_set = lax.dynamic_index_in_dim(set_index, own_seq, keepdims=False)
    low = order.reshape(2, half, 2)
    here = lax.dynamic_index_in_dim(low, place, 1, keepdims=False)
    flags = []
    for k in range(half):
        there = lax.dynamic_index_in_dim(low, place ^ k, 1, keepdims=False)
        flags.append((there[None, :, 0] < here[:, None, 0]).astype(jnp.int32).reshape(4))
    sc = jnp.concatenate(
        [jnp.stack([core, own_set, place, own_seq]).astype(jnp.int32), set_index] + flags
    )
    base = flag_base(n_seq)
    cos, sin = rope_tables(here.T.reshape(4))
    ones = jnp.asarray(np.kron(np.eye(4), np.ones((HEAD_SIZE, HEAD_SIZE))), bf16)
    gain_a = g_attn.astype(f32)[None]
    gain_f = g_ffn.astype(f32)[None]
    g_qk = jnp.concatenate(
        [jnp.tile(g_q, QW // HEAD_SIZE), jnp.tile(key_norm_gain, KW // HEAD_SIZE)]
    ).astype(f32)[None]
    a_qkv_t = jnp.swapaxes(a_qkv, 1, 2)
    a_o_t = jnp.swapaxes(a_o, 1, 2)
    a_gu_t = jnp.swapaxes(a_gu, 1, 2)
    a_down_t = jnp.swapaxes(a_down, 1, 2)

    u, raw, qm, kv = qkv_call(
        sc, mine, other, cos, sin, w_own, w_rec_q, w_rec_kv, gain_a, a_qkv_t, b_q, key_up_weight,
        value_up_weight, g_qk, ones,
    )
    kvs = [kv] + [partner(kv, k) for k in range(1, half)]
    acc = attend_call([base], sc, qm, [kv], None)
    cot = after(cot, mine)
    c_mine = jnp.where(stays, cot, swap(cot))
    c_sent = after(c_mine, acc)
    d_hid, ed, drdT = hidden_back_call(
        sc, c_mine, other_core(c_sent[:CH]), other_core(c_sent[CH:]), w_down, a_down_t, b_down
    )
    w_gu_late = after(w_gu, kv)
    gu_send = jnp.concatenate(
        [cols(w_gu_late, 0, HF, 1 - core), cols(w_gu_late, FF, HF, 1 - core)], axis=1
    )
    gu_rec = other_core(after(gu_send, d_hid, *kvs))
    acc = attend_call(
        [base + 4 * k for k in range(1, half)], sc, qm, kvs[1:], after(acc, d_hid, gu_send)
    )
    ob, mix, lse = project_call(sc, acc, w_o, a_o_t, b_o)
    mix_got = other_core(mix)
    y, down, du, pay_early = ffn_call(
        half, sc, mine, other, mix, mix_got, d_hid, ed, drdT, gain_f, w_gu, gu_rec, w_down,
        a_gu_t, b_gu, a_down_t, b_down,
    )
    dh, dom, delta, pay_early = back_mix_call(
        half, sc, mine, other, mix, mix_got, ed, du, other_core(du), gain_f, w_o, a_o_t, b_o, ob,
        ones, pay_early,
    )

    def summed(pay):
        shards = pay.reshape(half, -1, 128)
        total = shards[0].astype(f32)
        for k in range(1, half):
            total += partner(shards[k], k).astype(f32)
        return total.astype(bf16)

    dq = None
    got = []
    early = summed(pay_early)
    for k in list(range(1, half)) + [0]:
        dq, dkv = attend_back_call(base + 4 * k, k == 0, sc, qm, dom, kvs[k], lse, delta, dq)
        if k:
            got.append(partner(dkv, k))
        if k == half - 2:
            dq = after(dq, early)
    early = jnp.stack([early, other_seq(early, 1)])
    early = after(early, dq, *got)
    early_got = [early] + [partner(early, k) for k in range(1, half)]

    du_own, du_send, pay_late = qkv_back_call(
        half, sc, dq, dkv, got, raw, cos, sin, g_qk, ones, u, w_own, w_rec_q, w_rec_kv, a_qkv_t, b_q,
        key_up_weight, value_up_weight,
    )
    early = jnp.stack([after(v, pay_late) for v in early_got])
    early_got = [early] + [other_seq(early, 2 * d) for d in range(1, n_seq)]
    late = summed(pay_late)
    late = jnp.stack([late] + [other_seq(late, d) for d in range(1, 2 * n_seq)])
    early = jnp.stack([after(v, late) for v in early_got])
    early_twin = other_core(early)

    layer = y + other_core(after(down, dom)).astype(f32)
    stay_flag = stays.astype(jnp.int32).reshape(1)
    layer_out = home_call(stay_flag, layer, swap(layer.astype(bf16)))

    n_w = width // 128
    pieces = []
    for t in range(HF // 128):
        for q in range(2):
            pieces.append((t * 3 + q, 0, (q, slice(0, R)), t * 128, HF))
        pieces.append((t * 3 + 2, 1, (slice(0, R),), t * 128, HF))
    for t in range(n_w):
        pieces.append((GU_TILES + t, 2, (slice(0, R),), t * 128, 0))
        for q in range(2):
            rows_at = (slice(q * R, (q + 1) * R),)
            pieces.append((GU_TILES + n_w + t * 2 + q, 3, rows_at, t * 128, 0))
    for t in range(n_w):
        pieces.append((GU_TILES + 3 * n_w + t, 4, (slice(0, R),), t * 128, 0))
    for t in range(QW // 128):
        pieces.append((GU_TILES + 4 * n_w + t, 5, (slice(0, R),), t * 128, QW))
    r_gu, r_ad, r_bd, r_agu, r_bo, r_ao = place_call(
        pieces,
        [(2, R, FF), (R, FF), (R, width), (2 * R, width), (R, width), (R, 2 * QW)],
        n_seq, sc, early, early_twin,
    )

    late = jnp.stack([late] + [partner(late, k) for k in range(1, half)])[None]
    late_twin = after(other_core(late), r_gu)
    grad_in, grad_low = norm_back_call(mine, du_own, other_core(du_send), dh, gain_a)
    input_grad = home_call(stay_flag, grad_in, swap(grad_low))

    pieces = []
    first_rows = (slice(0, R),)
    for t in range(n_w):
        for q in range(3):
            pieces.append((t * 3 + q, 0, (slice(q * R, (q + 1) * R),), t * 128, 0))
    for t in range(EW // 128):
        at = 3 * n_w + t
        if t < QW // 128:
            pieces.append((at, 1, first_rows, t * 128, QW))
        elif t < (QW + KW) // 128:
            pieces.append((at, 2, first_rows, t * 128 - QW, KW))
        else:
            pieces.append((at, 3, first_rows, t * 128 - QW - KW, KW))
    r_aqkv, r_bq, r_bk, r_bv = place_call(
        pieces,
        [(3 * R, width), (R, 2 * QW), (R, 2 * KW), (R, 2 * KW)],
        n_seq, sc, late, late_twin,
    )
    return (
        layer_out,
        input_grad,
        jnp.swapaxes(r_aqkv, 1, 2),
        r_bq,
        r_bk,
        r_bv,
        jnp.swapaxes(r_ao, 1, 2),
        r_bo,
        jnp.swapaxes(r_agu, 1, 2),
        r_gu,
        jnp.swapaxes(r_ad, 1, 2),
        r_bd,
    )


def solution(mesh):
    tokens = P("ctx", ("seq", "wsh"), None)
    in_specs = (
        (tokens, tokens) + (P("wsh", None),) * 4 + (P(),) * 15 + (P(("seq", "wsh"), None),)
    )
    out_specs = (tokens, tokens) + (P(),) * 10
    return jax.shard_map(
        per_device, mesh=mesh, in_specs=in_specs, out_specs=out_specs, check_vma=False
    )
```

```python
import functools
import math

import jax
import jax.numpy as jnp
import numpy as np
from jax import lax
from jax.experimental import pallas as pl
from jax.experimental.pallas import tpu as pltpu
from jax.sharding import PartitionSpec as P

QUERY_HEADS = 16
KEY_VALUE_HEADS = 8
HEAD_SIZE = 64
FF = 4608
ADAPTER_RANK = 16
ADAPTER_SETS = 8
CH = 128

epsilon = 1e-05
rope_base = 1000000.0

TOK = 4 * CH
PAIR = 2 * HEAD_SIZE
QW = QUERY_HEADS * HEAD_SIZE // 2
KW = KEY_VALUE_HEADS * HEAD_SIZE // 2
EW = QW + 2 * KW
GROUPS = KEY_VALUE_HEADS // 2
HF = FF // 2
TF = 768
NT = HF // TF
R = ADAPTER_RANK
MIB = 1024 * 1024
f32 = jnp.float32
bf16 = jnp.bfloat16


def mm(a, b):
    return lax.dot_general(a, b, (((1,), (0,)), ((), ())), preferred_element_type=f32)


def mm_nt(a, b):
    return lax.dot_general(a, b, (((1,), (1,)), ((), ())), preferred_element_type=f32)


def params(mib):
    return pltpu.CompilerParams(
        dimension_semantics=("arbitrary",), vmem_limit_bytes=mib * MIB
    )


def cost(flops, nbytes):
    return pl.CostEstimate(flops=int(flops), bytes_accessed=int(nbytes), transcendentals=0)


def whole(shape):
    return pl.BlockSpec(shape, lambda *_: (0,) * len(shape))


def split_dot(x, ones):
    hi = x.astype(bf16)
    lo = (x - hi.astype(f32)).astype(bf16)
    return mm(hi, ones) + mm(lo, ones)


def head_mean(x, ones):
    width = ones.shape[0]
    parts = [
        split_dot(x[:, i : i + width], ones) for i in range(0, x.shape[1], width)
    ]
    return jnp.concatenate(parts, axis=1) * (1.0 / HEAD_SIZE)


def lane_iota(shape):
    return lax.broadcasted_iota(jnp.int32, shape, len(shape) - 1)


def half_turn(x):
    width = x.shape[1]
    near = pltpu.roll(x, HEAD_SIZE // 2, 1)
    far = pltpu.roll(x, width - HEAD_SIZE // 2, 1)
    return jnp.where(lane_iota(x.shape) % HEAD_SIZE < HEAD_SIZE // 2, far, near)


def widen(table, width):
    return jnp.concatenate([table] * (width // table.shape[1]), axis=1)


def put_masked(x, out):
    rows = x.shape[0]
    left = lane_iota((rows, PAIR)) < HEAD_SIZE
    for g in range(GROUPS):
        tile = x[:, g * PAIR : (g + 1) * PAIR]
        turned = pltpu.roll(tile, HEAD_SIZE, 1)
        if g % 2 == 0:
            pair = (jnp.where(left, tile, 0.0), jnp.where(left, turned, 0.0))
        else:
            pair = (jnp.where(left, 0.0, turned), jnp.where(left, 0.0, tile))
        for j in range(2):
            out[g, j * rows : (j + 1) * rows, :] = pair[j].astype(bf16)


def in_order(core, m, o):
    a = jnp.where(core == 0, m, o)
    b = jnp.where(core == 0, o, m)
    return jnp.concatenate([a[:CH], b[:CH], a[CH:], b[CH:]], axis=0)


def lanes_at(index, depth):
    return pl.ds(pl.multiple_of(index * depth, depth), depth)


def put_tile(sc, ref, per_shard, index, value):
    shard = (index // per_shard) ^ sc[2]
    row = shard * (per_shard * R) + (index % per_shard) * R
    ref[pl.ds(pl.multiple_of(row, R), R), :] = value.astype(ref.dtype)


def flag_base(n_seq):
    return 4 + 2 * n_seq


def qkv_kernel(
    sc, mine, other, cos, sin, w_own, w_rec_q, w_rec_kv, gain, a_t, b_q, b_k, b_v, g_qk, ones,
    u_out, raw_out, qm_out, kv_out, u_s, b_s,
):
    core = sc[0]
    a = jnp.where(core == 0, mine[0], other[0])
    b = jnp.where(core == 0, other[0], mine[0])
    x = jnp.concatenate([a, b], axis=0).astype(f32)
    inv = lax.rsqrt(jnp.mean(x * x, axis=1, keepdims=True) + epsilon)
    u = (x * inv * gain[...]).astype(bf16)
    u_s[...] = u
    u_out[...] = u
    depth = w_own.shape[0]

    @pl.when(pl.program_id(0) == 0)
    def _():
        b_s[...] = jnp.zeros_like(b_s)
        b_s[0:R, 0:QW] = b_q[0]
        b_s[R : 2 * R, QW : QW + KW] = b_k[0]
        b_s[2 * R : 3 * R, QW + KW : EW] = b_v[0]

    rank = mm_nt(u, a_t[0]).astype(bf16)
    raw = mm(u_s[:, lanes_at(core, depth)], w_own[...])
    u_rec = u_s[:, lanes_at(1 - core, depth)]
    raw += jnp.concatenate([mm(u_rec, w_rec_q[...]), mm(u_rec, w_rec_kv[...])], axis=1)
    raw += mm(rank, b_s[...])
    qk = raw[:, : QW + KW]
    raw_out[...] = qk
    normed = qk * lax.rsqrt(head_mean(qk * qk, ones[...]) + epsilon) * g_qk[...]
    turned = normed * widen(cos[...], QW + KW) + half_turn(normed) * widen(sin[...], QW + KW)

    put_masked(turned[:, :QW] * (1.0 / math.sqrt(HEAD_SIZE)), qm_out)
    kv_out[...] = jnp.concatenate([turned[:, QW:], raw[:, QW + KW :]], axis=1).astype(bf16)


def qkv_call(sc, mine, other, cos, sin, w_own, w_rec_q, w_rec_kv, gain, a_t, b_q, b_k, b_v, g_qk, ones):
    rows, width = mine.shape
    depth = w_own.shape[0]
    n = TOK // 2

    def rows_spec(cols):
        return pl.BlockSpec((n, cols), lambda i, s: (i, 0))

    half_spec = pl.BlockSpec((1, rows // 2, width), lambda i, s: (i, 0, 0))
    return pl.pallas_call(
        qkv_kernel,
        grid_spec=pltpu.PrefetchScalarGridSpec(
            num_scalar_prefetch=1,
            grid=(2,),
            in_specs=[
                half_spec, half_spec,
                rows_spec(PAIR), rows_spec(PAIR),
                whole((depth, EW)), whole((depth, QW)), whole((depth, 2 * KW)),
                whole((1, width)),
                pl.BlockSpec((1, 3 * R, width), lambda i, s: (s[1], 0, 0)),
                pl.BlockSpec((1, R, QW), lambda i, s: (s[1], 0, s[0])),
                pl.BlockSpec((1, R, KW), lambda i, s: (s[1], 0, s[0])),
                pl.BlockSpec((1, R, KW), lambda i, s: (s[1], 0, s[0])),
                whole((1, QW + KW)), whole(ones.shape),
            ],
            out_specs=[
                rows_spec(width), rows_spec(QW + KW),
                pl.BlockSpec((GROUPS, TOK, PAIR), lambda i, s: (0, i, 0)),
                rows_spec(2 * KW),
            ],
            scratch_shapes=[pltpu.VMEM((n, width), bf16), pltpu.VMEM((3 * R, EW), bf16)],
        ),
        out_shape=[
            jax.ShapeDtypeStruct((TOK, width), bf16),
            jax.ShapeDtypeStruct((TOK, QW + KW), f32),
            jax.ShapeDtypeStruct((GROUPS, 2 * TOK, PAIR), bf16),
            jax.ShapeDtypeStruct((TOK, 2 * KW), bf16),
        ],
        compiler_params=params(20),
        cost_estimate=cost(1e8, 1e6),
        name="qkv",
    )(
        sc, mine.reshape(2, rows // 2, width), other.reshape(2, rows // 2, width), cos, sin,
        w_own, w_rec_q, w_rec_kv, gain, a_t, b_q, b_k, b_v, g_qk, ones,
    )


def block_mask(sc, base, first, high, keys_first):
    shape = (2 * CH, 2 * CH)
    row = lax.broadcasted_iota(jnp.int32, shape, 0)
    col = lax.broadcasted_iota(jnp.int32, shape, 1)
    q, k = (col, row) if keys_first else (row, col)

    def pick(qb, kb):
        if first and qb == kb:
            return (k <= q).astype(f32)
        flag = sc[base + qb * 2 + kb]
        flag = 1 - flag if high else flag
        return flag.astype(f32)

    by_key = [jnp.where(k < CH, pick(qb, 0), pick(qb, 1)) for qb in range(2)]
    return jnp.where(q < CH, by_key[0], by_key[1])


def attend_kernel(bases, first, sc, qm, *rest):
    kvs = rest[: 2 * len(bases)]
    if first:
        acc_out, mask, vx = rest[2 * len(bases) :]
    else:
        acc_in, acc_out, mask, vx = rest[2 * len(bases) :]
    g = pl.program_id(0)
    n = 2 * CH

    @pl.when(g == 0)
    def _():
        for i, base in enumerate(bases):
            mask[i, 0] = block_mask(sc, base, first, False, False).astype(bf16)
            mask[i, 1] = block_mask(sc, base, first, True, False).astype(bf16)
        vx[:, :, PAIR:] = jnp.ones((len(bases), TOK, PAIR), bf16)

    o_low = o_high = None
    for i in range(len(bases)):
        k, v = kvs[2 * i], kvs[2 * i + 1]
        vx[i, :, :PAIR] = v[...]
        s_high = mm_nt(qm[0, 2 * n :, :], k[...])
        s_low = mm_nt(qm[0, : 2 * n, :], k[:n, :])
        p_all = jnp.exp(s_high[:, :n]).astype(bf16)
        p_high = jnp.exp(s_high[:, n:]).astype(bf16)
        p_low = jnp.exp(s_low).astype(bf16)
        m_low, m_high = mask[i, 0], mask[i, 1]
        p_high = jnp.concatenate([p_high[:n] * m_high, p_high[n:] * m_high], axis=0)
        p_low = jnp.concatenate([p_low[:n] * m_low, p_low[n:] * m_low], axis=0)
        high = mm(jnp.concatenate([p_all, p_high], axis=1), vx[i])
        low = mm(p_low, vx[i, :n, :])
        o_high = high if i == 0 else o_high + high
        o_low = low if i == 0 else o_low + low
    left = lane_iota((n, PAIR)) < HEAD_SIZE
    even = g % 2 == 0
    for lh, o in ((0, o_low), (1, o_high)):
        rows = slice(lh * n, (lh + 1) * n)
        o0, o1 = o[:n, :PAIR], o[n:, :PAIR]
        move = pltpu.roll(jnp.where(even, o1, o0), HEAD_SIZE, 1)
        value = jnp.where(left, jnp.where(even, o0, move), jnp.where(even, move, o1))
        norm = jnp.where(left, o[:n, PAIR:], o[n:, PAIR:])
        if not first:
            value += acc_in[0, rows, :PAIR]
            norm += acc_in[0, rows, PAIR:]
        acc_out[0, rows, :PAIR] = value
        acc_out[0, rows, PAIR:] = norm


def attend_call(bases, sc, qm, kvs, acc):
    first = acc is None
    acc_spec = pl.BlockSpec((1, TOK, 2 * PAIR), lambda g, s: (g, 0, 0))
    kv_specs = [
        pl.BlockSpec((TOK, PAIR), lambda g, s: (0, g // 2)),
        pl.BlockSpec((TOK, PAIR), lambda g, s: (0, GROUPS // 2 + g // 2)),
    ]
    n = len(bases)
    return pl.pallas_call(
        functools.partial(attend_kernel, bases, first),
        grid_spec=pltpu.PrefetchScalarGridSpec(
            num_scalar_prefetch=1,
            grid=(GROUPS,),
            in_specs=[pl.BlockSpec((1, 2 * TOK, PAIR), lambda g, s: (g, 0, 0))]
            + kv_specs * n
            + ([] if first else [acc_spec]),
            out_specs=acc_spec,
            scratch_shapes=[
                pltpu.VMEM((n, 2, 2 * CH, 2 * CH), bf16),
                pltpu.VMEM((n, TOK, 2 * PAIR), bf16),
            ],
        ),
        out_shape=jax.ShapeDtypeStruct((GROUPS, TOK, 2 * PAIR), f32),
        input_output_aliases={} if first else {2 + 2 * n: 0},
        compiler_params=params(12 if n < 8 else 40),
        cost_estimate=cost(1e8, 1e6),
        name="attend",
    )(sc, qm, *[kv for kv in kvs for _ in range(2)], *([] if first else [acc]))


def head_lines(tiles, out):
    rows = tiles[0].shape[0]
    lane = lane_iota(tiles[0].shape) % HEAD_SIZE
    packed = tiles[0]
    for g in range(1, GROUPS):
        packed = jnp.where(lane == g, tiles[g], packed)
    turned = packed.T
    for g in range(GROUPS):
        for j in range(2):
            row = j * HEAD_SIZE + g
            out[g, :, j * rows : (j + 1) * rows] = turned[row : row + 1, :]


def project_kernel(sc, acc, w_o, a_o, b_o, ob_out, mix_out, lse_out):
    parts, norms = [], []
    for g in range(GROUPS):
        norm = acc[g, :, PAIR:]
        parts.append(acc[g, :, :PAIR] / norm)
        norms.append(norm)
    ob = jnp.concatenate(parts, axis=1).astype(bf16)
    ob_out[...] = ob
    head_lines(norms, lse_out)
    lse_out[...] = jnp.log(lse_out[...])
    rank = mm_nt(ob, a_o[0]).astype(bf16)
    mix_out[...] = (mm(ob, w_o[...]) + mm(rank, b_o[0])).astype(bf16)


def project_call(sc, acc, w_o, a_o, b_o):
    width = w_o.shape[1]
    n = TOK // 2
    return pl.pallas_call(
        project_kernel,
        grid_spec=pltpu.PrefetchScalarGridSpec(
            num_scalar_prefetch=1,
            grid=(2,),
            in_specs=[
                pl.BlockSpec((GROUPS, n, 2 * PAIR), lambda i, s: (0, i, 0)),
                whole(w_o.shape),
                pl.BlockSpec((1, R, QW), lambda i, s: (s[1], 0, s[0])),
                pl.BlockSpec((1, R, width), lambda i, s: (s[1], 0, 0)),
            ],
            out_specs=[
                pl.BlockSpec((n, QW), lambda i, s: (i, 0)),
                pl.BlockSpec((n, width), lambda i, s: (i, 0)),
                pl.BlockSpec((GROUPS, 1, 2 * n), lambda i, s: (0, 0, i)),
            ],
        ),
        out_shape=[
            jax.ShapeDtypeStruct((TOK, QW), bf16),
            jax.ShapeDtypeStruct((TOK, width), bf16),
            jax.ShapeDtypeStruct((GROUPS, 1, 2 * TOK), f32),
        ],
        compiler_params=params(14),
        cost_estimate=cost(1e8, 1e6),
        name="project",
    )(sc, acc, w_o, a_o, b_o)


def hidden_back_kernel(sc, c_mine, c_low, c_high, w_d, a_d, b_d, out, ed_out, drT_out, ed_s, dr_s):
    @pl.when(pl.program_id(0) == 0)
    def _():
        c_other = jnp.concatenate([c_low[...], c_high[...]], axis=0)
        ed = in_order(sc[0], c_mine[...], c_other)
        ed_s[...] = ed
        ed_out[...] = ed
        dr_s[...] = mm_nt(ed, b_d[0]).astype(bf16)
        drT_out[...] = mm_nt(b_d[0], ed).astype(bf16)

    out[...] = mm_nt(ed_s[...], w_d[...]) + mm(dr_s[...], a_d[0])


def hidden_back_call(sc, c_mine, c_low, c_high, w_d, a_d, b_d):
    rows, width = c_mine.shape
    return pl.pallas_call(
        hidden_back_kernel,
        grid_spec=pltpu.PrefetchScalarGridSpec(
            num_scalar_prefetch=1,
            grid=(NT,),
            in_specs=[
                whole((rows, width)), whole((CH, width)), whole((CH, width)),
                pl.BlockSpec((TF, width), lambda i, s: (i, 0)),
                pl.BlockSpec((1, R, TF), lambda i, s: (s[1], 0, s[0] * NT + i)),
                pl.BlockSpec((1, R, width), lambda i, s: (s[1], 0, 0)),
            ],
            out_specs=[
                pl.BlockSpec((TOK, TF), lambda i, s: (0, i)), whole((TOK, width)), whole((R, TOK)),
            ],
            scratch_shapes=[pltpu.VMEM((TOK, width), bf16), pltpu.VMEM((TOK, R), bf16)],
        ),
        out_shape=[
            jax.ShapeDtypeStruct((TOK, HF), f32),
            jax.ShapeDtypeStruct((TOK, width), bf16),
            jax.ShapeDtypeStruct((R, TOK), bf16),
        ],
        compiler_params=params(20),
        cost_estimate=cost(1e8, 1e6),
        name="hidden_back",
    )(sc, c_mine, c_low, c_high, w_d, a_d, b_d)


GU_TILES = 3 * HF // 128


def early_tiles(width):
    return GU_TILES + 4 * width // 128 + QW // 128


def ffn_kernel(
    per_shard,
    sc, mine, other, mix_a, mix_b, dh_tile, ed, drdT, gain, wg_own, wu_own, wg_rec, wu_rec, w_d,
    a_gu, b_gu, a_d, b_d,
    y_out, down_out, du_out, pay,
    u_s, down_s, du_s, rgu_s, rguT_s, rdT_s, drguT_s,
):
    i = pl.program_id(0)
    core = sc[0]
    depth = wg_own.shape[0]
    width = u_s.shape[1]
    own = lanes_at(core, depth)
    rec = lanes_at(1 - core, depth)

    @pl.when(i == 0)
    def _():
        x = in_order(core, mine[...], other[...]).astype(f32)
        h = x + (mix_a[...].astype(f32) + mix_b[...].astype(f32))
        inv = lax.rsqrt(jnp.mean(h * h, axis=1, keepdims=True) + epsilon)
        u = (h * inv * gain[...]).astype(bf16)
        u_s[...] = u
        rgu_s[...] = mm_nt(u, a_gu[0]).astype(bf16)
        rguT_s[...] = mm_nt(a_gu[0], u).astype(bf16)
        rdT_s[...] = jnp.zeros_like(rdT_s)
        drguT_s[...] = jnp.zeros_like(drguT_s)
        pay[...] = jnp.zeros_like(pay)

    u_own, u_rec = u_s[:, own], u_s[:, rec]
    hids, egs, eus = [], [], []
    for n in range(TF // 256):
        at = slice(n * 256, (n + 1) * 256)
        gate = mm(u_own, wg_own[:, at]) + mm(u_rec, wg_rec[:, at]) + mm(rgu_s[:, :R], b_gu[0, 0, :, at])
        up = mm(u_own, wu_own[:, at]) + mm(u_rec, wu_rec[:, at]) + mm(rgu_s[:, R:], b_gu[0, 1, :, at])
        d_hid = dh_tile[:, at]
        sig = 0.5 + 0.5 * jnp.tanh(0.5 * gate)
        silu = gate * sig
        hids.append((silu * up).astype(bf16))
        egs.append((d_hid * up * (sig + (silu - silu * sig))).astype(bf16))
        eus.append((d_hid * silu).astype(bf16))
    hid, e_g, e_u = [jnp.concatenate(v, axis=1) for v in (hids, egs, eus)]
    down = mm(hid, w_d[...])
    du_own = mm_nt(e_g, wg_own[...]) + mm_nt(e_u, wu_own[...])
    du_rec = mm_nt(e_g, wg_rec[...]) + mm_nt(e_u, wu_rec[...])

    @pl.when(i == 0)
    def _():
        down_s[...] = down
        du_s[:, own] = du_own
        du_s[:, rec] = du_rec

    @pl.when(i > 0)
    def _():
        down_s[...] += down
        du_s[:, own] += du_own
        du_s[:, rec] += du_rec

    rdT_s[...] += mm_nt(a_d[0], hid)
    drguT_s[:R, :] += mm_nt(b_gu[0, 0], e_g)
    drguT_s[R:, :] += mm_nt(b_gu[0, 1], e_u)
    grads = (mm(rguT_s[:R], e_g), mm(rguT_s[R:], e_u), mm(drdT[...], hid))
    for t in range(TF // 128):
        for q in range(3):
            index = (i * (TF // 128) + t) * 3 + q
            put_tile(sc, pay, per_shard, index, grads[q][:, t * 128 : (t + 1) * 128])

    @pl.when(i == pl.num_programs(0) - 1)
    def _():
        rdT = rdT_s[...].astype(bf16)
        drT = drguT_s[...].astype(bf16)
        tn = (((0,), (0,)), ((), ()))
        down_s[...] += lax.dot_general(rdT, b_d[0], tn, preferred_element_type=f32)
        du_out[...] = (
            du_s[...] + lax.dot_general(drT, a_gu[0], tn, preferred_element_type=f32)
        ).astype(bf16)
        for lh in range(2):
            at = slice(lh * CH, (lh + 1) * CH)
            row = pl.ds(pl.multiple_of(lh * 2 * CH + core * CH, CH), CH)
            out = pl.ds(pl.multiple_of(lh * 2 * CH + (1 - core) * CH, CH), CH)
            mix = mix_a[row, :].astype(f32) + mix_b[row, :].astype(f32)
            y_out[at, :] = (mine[at, :].astype(f32) + mix) + down_s[row, :]
            down_out[at, :] = down_s[out, :].astype(bf16)
        gb = mm(rdT, ed[...])
        ga = mm(drT, u_s[...])
        for t in range(width // 128):
            at = slice(t * 128, (t + 1) * 128)
            put_tile(sc, pay, per_shard, GU_TILES + t, gb[:, at])
            for q in range(2):
                index = GU_TILES + width // 128 + t * 2 + q
                put_tile(sc, pay, per_shard, index, ga[q * R : (q + 1) * R, at])


def ffn_call(
    half, sc, mine, other, mix_a, mix_b, d_hid, ed, drdT, gain, w_gu, w_rec, w_d, a_gu, b_gu,
    a_d, b_d,
):
    rows, width = mine.shape
    depth = w_gu.shape[0]
    per_shard = -(-early_tiles(width) // half)
    block = whole((rows, width))
    full = whole((TOK, width))
    return pl.pallas_call(
        functools.partial(ffn_kernel, per_shard),
        grid_spec=pltpu.PrefetchScalarGridSpec(
            num_scalar_prefetch=1,
            grid=(NT,),
            in_specs=[
                block, block, full, full,
                pl.BlockSpec((TOK, TF), lambda i, s: (0, i)),
                full, whole((R, TOK)), whole((1, width)),
                pl.BlockSpec((depth, TF), lambda i, s: (0, s[0] * NT + i)),
                pl.BlockSpec((depth, TF), lambda i, s: (0, 2 * NT + s[0] * NT + i)),
                pl.BlockSpec((depth, TF), lambda i, s: (0, i)),
                pl.BlockSpec((depth, TF), lambda i, s: (0, NT + i)),
                pl.BlockSpec((TF, width), lambda i, s: (i, 0)),
                pl.BlockSpec((1, 2 * R, width), lambda i, s: (s[1], 0, 0)),
                pl.BlockSpec((1, 2, R, TF), lambda i, s: (s[1], 0, 0, s[0] * NT + i)),
                pl.BlockSpec((1, R, TF), lambda i, s: (s[1], 0, s[0] * NT + i)),
                pl.BlockSpec((1, R, width), lambda i, s: (s[1], 0, 0)),
            ],
            out_specs=[block, block, full, whole((half * per_shard * R, 128))],
            scratch_shapes=[
                pltpu.VMEM((TOK, width), bf16),
                pltpu.VMEM((TOK, width), f32),
                pltpu.VMEM((TOK, width), f32),
                pltpu.VMEM((TOK, 2 * R), bf16),
                pltpu.VMEM((2 * R, TOK), bf16),
                pltpu.VMEM((R, TOK), f32),
                pltpu.VMEM((2 * R, TOK), f32),
            ],
        ),
        out_shape=[
            jax.ShapeDtypeStruct((rows, width), f32),
            jax.ShapeDtypeStruct((rows, width), bf16),
            jax.ShapeDtypeStruct((TOK, width), bf16),
            jax.ShapeDtypeStruct((half * per_shard * R, 128), bf16),
        ],
        compiler_params=params(40),
        cost_estimate=cost(1e9, 2.5e6),
        name="ffn",
    )(
        sc, mine, other, mix_a, mix_b, d_hid, ed, drdT, gain, w_gu, w_gu, w_rec, w_rec, w_d,
        a_gu, b_gu, a_d, b_d,
    )


def back_mix_kernel(
    per_shard,
    sc, mine, other, mix_a, mix_b, ed, du_a, du_b, gain, w_o, a_o, b_o, ob, ones, pay_in,
    dh_out, dom_out, delta_out, pay, dh_s, gb_s, ga_s,
):
    i = pl.program_id(0)
    core = sc[0]

    def pair(m, o):
        a = jnp.where(core == 0, m[0], o[0])
        b = jnp.where(core == 0, o[0], m[0])
        return jnp.concatenate([a, b], axis=0).astype(f32)

    hv = pair(mine, other) + (mix_a[...].astype(f32) + mix_b[...].astype(f32))
    inv = lax.rsqrt(jnp.mean(hv * hv, axis=1, keepdims=True) + epsilon)
    w = gain[...] * (du_a[...].astype(f32) + du_b[...].astype(f32))
    dh = ed[...].astype(f32) + inv * w - hv * (
        inv * inv * inv * jnp.mean(hv * w, axis=1, keepdims=True)
    )
    dh_s[...] = dh
    dh_out[...] = dh_s[pl.ds(pl.multiple_of(core * CH, CH), CH), :]
    e_o = dh.astype(bf16)
    obv = ob[...]
    dr = mm_nt(e_o, b_o[0]).astype(bf16)
    drT = mm_nt(b_o[0], e_o).astype(bf16)
    rT = mm_nt(a_o[0], obv).astype(bf16)
    gb = mm(rT, e_o)
    ga = mm(drT, obv)

    @pl.when(i == 0)
    def _():
        gb_s[...] = gb
        ga_s[...] = ga

    @pl.when(i > 0)
    def _():
        gb_s[...] += gb
        ga_s[...] += ga
        pay[...] = pay_in[...]
        n_w = dh_s.shape[1] // 128
        for t in range(n_w):
            index = GU_TILES + 3 * n_w + t
            put_tile(sc, pay, per_shard, index, gb_s[:, t * 128 : (t + 1) * 128])
        for t in range(QW // 128):
            index = GU_TILES + 4 * n_w + t
            put_tile(sc, pay, per_shard, index, ga_s[:, t * 128 : (t + 1) * 128])

    d_o = (mm_nt(e_o, w_o[...]) + mm(dr, a_o[0])).astype(bf16).astype(f32)
    prod = head_mean(d_o * obv.astype(f32), ones[...]) * HEAD_SIZE
    head_lines([prod[:, g * PAIR : (g + 1) * PAIR] for g in range(GROUPS)], delta_out)
    put_masked(d_o, dom_out)


def back_mix_call(
    half, sc, mine, other, mix_a, mix_b, ed, du_a, du_b, gain, w_o, a_o, b_o, ob, ones, pay,
):
    rows, width = mine.shape
    per_shard = -(-early_tiles(width) // half)
    n = TOK // 2
    block = pl.BlockSpec((1, rows // 2, width), lambda i, s: (i, 0, 0))
    full = pl.BlockSpec((n, width), lambda i, s: (i, 0))

    def two(v):
        return v.reshape(2, rows // 2, width)

    return pl.pallas_call(
        functools.partial(back_mix_kernel, per_shard),
        grid_spec=pltpu.PrefetchScalarGridSpec(
            num_scalar_prefetch=1,
            grid=(2,),
            in_specs=[
                block, block, full, full, full, full, full,
                whole((1, width)), whole(w_o.shape),
                pl.BlockSpec((1, R, QW), lambda i, s: (s[1], 0, s[0])),
                pl.BlockSpec((1, R, width), lambda i, s: (s[1], 0, 0)),
                pl.BlockSpec((n, QW), lambda i, s: (i, 0)),
                whole(ones.shape), whole(pay.shape),
            ],
            out_specs=[
                pl.BlockSpec((rows // 2, width), lambda i, s: (i, 0)),
                pl.BlockSpec((GROUPS, TOK, PAIR), lambda i, s: (0, i, 0)),
                pl.BlockSpec((GROUPS, 1, 2 * n), lambda i, s: (0, 0, i)),
                whole(pay.shape),
            ],
            scratch_shapes=[
                pltpu.VMEM((n, width), f32), pltpu.VMEM((R, width), f32), pltpu.VMEM((R, QW), f32),
            ],
        ),
        out_shape=[
            jax.ShapeDtypeStruct((rows, width), f32),
            jax.ShapeDtypeStruct((GROUPS, 2 * TOK, PAIR), bf16),
            jax.ShapeDtypeStruct((GROUPS, 1, 2 * TOK), f32),
            jax.ShapeDtypeStruct(pay.shape, pay.dtype),
        ],
        input_output_aliases={14: 3},
        compiler_params=params(24),
        cost_estimate=cost(1e8, 1e6),
        name="back_mix",
    )(
        sc, two(mine), two(other), mix_a, mix_b, ed, du_a, du_b, gain,
        w_o, a_o, b_o, ob, ones, pay,
    )


def attend_back_kernel(base, first, has_dq, sc, qm, dom, k, v, lse, delta, *rest):
    if has_dq:
        dq_in, dq_out, dkv_out, dkv, kt, mask = rest
    else:
        dq_out, dkv_out, dkv, kt, mask = rest
    g = pl.program_id(0)
    side = g % 2
    n = 2 * CH

    @pl.when(g == 0)
    def _():
        mask[0] = block_mask(sc, base, first, False, True)
        mask[1] = block_mask(sc, base, first, True, True)

    @pl.when(side == 0)
    def _():
        kt[...] = k[...].astype(f32).T.astype(bf16)

    kth = kt.at[pl.ds(pl.multiple_of(side * HEAD_SIZE, HEAD_SIZE), HEAD_SIZE), :]
    q_all, do_all = qm[0], dom[0]
    q_high, do_high = qm[0, 2 * n :, :], dom[0, 2 * n :, :]
    s_low = mm_nt(k[:n, :], q_all)
    s_high = mm_nt(k[n:, :], q_high)
    dp_low = mm_nt(v[:n, :], do_all)
    dp_high = mm_nt(v[n:, :], do_high)
    m_low, m_high = mask[0], mask[1]
    lse_all, delta_all = lse[0], delta[0]
    p_low = jnp.exp(s_low - lse_all)
    p_low = jnp.concatenate(
        [p_low[:, :n] * m_low, p_low[:, n : 2 * n] * m_low, p_low[:, 2 * n :]], axis=1
    )
    p_high = jnp.exp(s_high - lse_all[:, 2 * n :])
    p_high = jnp.concatenate([p_high[:, :n] * m_high, p_high[:, n:] * m_high], axis=1)
    ds_low = (p_low * (dp_low - delta_all)).astype(bf16)
    ds_high = (p_high * (dp_high - delta_all[:, 2 * n :])).astype(bf16)
    p_low, p_high = p_low.astype(bf16), p_high.astype(bf16)
    dk_low, dk_high = mm(ds_low, q_all), mm(ds_high, q_high)
    dv_low, dv_high = mm(p_low, do_all), mm(p_high, do_high)
    dq_low = mm(kth[:, :n], ds_low)
    dq_high = mm(kth[:, n:], ds_high)
    dq = jnp.concatenate([dq_low[:, : 2 * n], dq_low[:, 2 * n :] + dq_high], axis=1)
    dq_out[0] = dq_in[0] + dq if has_dq else dq

    @pl.when(side == 0)
    def _():
        dkv[0, :n, :] = dk_low
        dkv[0, n:, :] = dk_high
        dkv[1, :n, :] = dv_low
        dkv[1, n:, :] = dv_high

    @pl.when(side == 1)
    def _():
        dkv_out[0, :n, :] = (dkv[0, :n, :] + dk_low).astype(dkv_out.dtype)
        dkv_out[0, n:, :] = (dkv[0, n:, :] + dk_high).astype(dkv_out.dtype)
        dkv_out[1, :n, :] = (dkv[1, :n, :] + dv_low).astype(dkv_out.dtype)
        dkv_out[1, n:, :] = (dkv[1, n:, :] + dv_high).astype(dkv_out.dtype)


def attend_back_call(base, first, sc, qm, dom, kv, lse, delta, dq):
    has_dq = dq is not None
    dq_spec = pl.BlockSpec((1, HEAD_SIZE, 2 * TOK), lambda g, s: (g, 0, 0))
    row_spec = pl.BlockSpec((1, 1, 2 * TOK), lambda g, s: (g, 0, 0))
    return pl.pallas_call(
        functools.partial(attend_back_kernel, base, first, has_dq),
        grid_spec=pltpu.PrefetchScalarGridSpec(
            num_scalar_prefetch=1,
            grid=(GROUPS,),
            in_specs=[
                pl.BlockSpec((1, 2 * TOK, PAIR), lambda g, s: (g, 0, 0)),
                pl.BlockSpec((1, 2 * TOK, PAIR), lambda g, s: (g, 0, 0)),
                pl.BlockSpec((TOK, PAIR), lambda g, s: (0, g // 2)),
                pl.BlockSpec((TOK, PAIR), lambda g, s: (0, GROUPS // 2 + g // 2)),
                row_spec, row_spec,
            ]
            + ([dq_spec] if has_dq else []),
            out_specs=[dq_spec, pl.BlockSpec((2, TOK, PAIR), lambda g, s: (0, 0, g // 2))],
            scratch_shapes=[
                pltpu.VMEM((2, TOK, PAIR), f32),
                pltpu.VMEM((PAIR, TOK), bf16),
                pltpu.VMEM((2, 2 * CH, 2 * CH), f32),
            ],
        ),
        out_shape=[
            jax.ShapeDtypeStruct((GROUPS, HEAD_SIZE, 2 * TOK), f32),
            jax.ShapeDtypeStruct((2, TOK, KW), f32 if first else bf16),
        ],
        input_output_aliases={7: 0} if has_dq else {},
        compiler_params=params(16),
        cost_estimate=cost(1e8, 1e6),
        name="attend_back",
    )(sc, qm, dom, kv, kv, lse, delta, *([dq] if has_dq else []))


def late_tiles(width):
    return 4 * width // 128


def qkv_back_kernel(per_shard, parts, sc, dq, dkv, *rest):
    got = rest[:parts]
    (raw, cos, sin, g_qk, ones, u, w_own, w_rec_q, w_rec_kv, a_t, b_q, b_k, b_v,
     du_out, send_out, pay, e_s, b_s, du_s, ga_s, gb_s) = rest[parts:]
    i = pl.program_id(0)
    core = sc[0]
    width = QW + KW

    @pl.when(i == 0)
    def _():
        b_s[...] = jnp.zeros_like(b_s)
        b_s[0:R, 0:QW] = b_q[0]
        b_s[R : 2 * R, QW:width] = b_k[0]
        b_s[2 * R : 3 * R, width:EW] = b_v[0]
        ga_s[...] = jnp.zeros_like(ga_s)
        gb_s[...] = jnp.zeros_like(gb_s)
        pay[...] = jnp.zeros_like(pay)

    m = dq.shape[2] // 2
    heads = [dq[g, :, j * m : (j + 1) * m] for g in range(GROUPS) for j in range(2)]
    d_q = jnp.concatenate(heads, axis=0).T * (1.0 / math.sqrt(HEAD_SIZE))
    d_k, d_v = dkv[0], dkv[1]
    for n in range(parts):
        d_k = d_k + got[n][0].astype(f32)
        d_v = d_v + got[n][1].astype(f32)
    grad = jnp.concatenate([d_q, d_k], axis=1)
    grad = grad * widen(cos[...], width) - half_turn(grad) * widen(sin[...], width)
    v = raw[...]
    inv = lax.rsqrt(head_mean(v * v, ones[...]) + epsilon)
    w = grad * g_qk[...]
    grad = inv * w - v * (inv * inv * inv) * head_mean(v * w, ones[...])
    e_s[:, :width] = grad.astype(bf16)
    e_s[:, width:] = d_v.astype(bf16)
    e = e_s[...]
    uv = u[...]
    dr = mm_nt(e, b_s[...]).astype(bf16)
    drT = mm_nt(b_s[...], e).astype(bf16)
    rT = mm_nt(a_t[0], uv).astype(bf16)
    gb_s[...] += mm(rT, e)
    ga_s[...] += mm(drT, uv)
    depth = w_own.shape[0]
    du_s[...] = mm(dr, a_t[0])
    du_s[:, lanes_at(core, depth)] += mm_nt(e, w_own[...])
    du_s[:, lanes_at(1 - core, depth)] += mm_nt(e[:, :QW], w_rec_q[...]) + mm_nt(
        e[:, QW:], w_rec_kv[...]
    )
    du_out[...] = du_s[pl.ds(pl.multiple_of(core * CH, CH), CH), :]
    send_out[...] = du_s[pl.ds(pl.multiple_of((1 - core) * CH, CH), CH), :].astype(bf16)

    @pl.when(i == pl.num_programs(0) - 1)
    def _():
        n = uv.shape[1] // 128
        for t in range(n):
            at = slice(t * 128, (t + 1) * 128)
            for q in range(3):
                put_tile(sc, pay, per_shard, t * 3 + q, ga_s[q * R : (q + 1) * R, at])
        for t in range(EW // 128):
            at = slice(t * 128, (t + 1) * 128)
            q = 0 if t < QW // 128 else (1 if t < width // 128 else 2)
            put_tile(sc, pay, per_shard, 3 * n + t, gb_s[q * R : (q + 1) * R, at])


def qkv_back_call(
    half, sc, dq, dkv, got, raw, cos, sin, g_qk, ones, u, w_own, w_rec_q, w_rec_kv, a_t, b_q, b_k,
    b_v,
):
    width = u.shape[1]
    depth = w_own.shape[0]
    parts = len(got)
    n = TOK // 2
    per_shard = -(-late_tiles(width) // half)

    def rows_spec(cols):
        return pl.BlockSpec((n, cols), lambda i, s: (i, 0))

    dkv_spec = pl.BlockSpec((2, n, KW), lambda i, s: (0, i, 0))
    half_spec = pl.BlockSpec((CH, width), lambda i, s: (i, 0))
    return pl.pallas_call(
        functools.partial(qkv_back_kernel, per_shard, parts),
        grid_spec=pltpu.PrefetchScalarGridSpec(
            num_scalar_prefetch=1,
            grid=(2,),
            in_specs=[pl.BlockSpec((GROUPS, HEAD_SIZE, 2 * n), lambda i, s: (0, 0, i)), dkv_spec]
            + [dkv_spec] * parts
            + [
                rows_spec(QW + KW), rows_spec(PAIR), rows_spec(PAIR), whole(g_qk.shape),
                whole(ones.shape), rows_spec(width), whole(w_own.shape),
                whole(w_rec_q.shape), whole(w_rec_kv.shape),
                pl.BlockSpec((1, 3 * R, width), lambda i, s: (s[1], 0, 0)),
                pl.BlockSpec((1, R, QW), lambda i, s: (s[1], 0, s[0])),
                pl.BlockSpec((1, R, KW), lambda i, s: (s[1], 0, s[0])),
                pl.BlockSpec((1, R, KW), lambda i, s: (s[1], 0, s[0])),
            ],
            out_specs=[half_spec, half_spec, whole((half * per_shard * R, 128))],
            scratch_shapes=[
                pltpu.VMEM((n, EW), bf16), pltpu.VMEM((3 * R, EW), bf16),
                pltpu.VMEM((n, width), f32), pltpu.VMEM((3 * R, width), f32),
                pltpu.VMEM((3 * R, EW), f32),
            ],
        ),
        out_shape=[
            jax.ShapeDtypeStruct((TOK // 2, width), f32),
            jax.ShapeDtypeStruct((TOK // 2, width), bf16),
            jax.ShapeDtypeStruct((half * per_shard * R, 128), bf16),
        ],
        compiler_params=params(24),
        cost_estimate=cost(1e8, 1e6),
        name="qkv_back",
    )(
        sc, dq, dkv, *got, raw, cos, sin, g_qk, ones, u, w_own, w_rec_q, w_rec_kv, a_t, b_q, b_k,
        b_v,
    )


def norm_back_kernel(x, du, got, dh, gain, out, low_out):
    v = x[...].astype(f32)
    inv = lax.rsqrt(jnp.mean(v * v, axis=1, keepdims=True) + epsilon)
    w = (du[...] + got[...].astype(f32)) * gain[...]
    grad = dh[...] + inv * w - v * (inv * inv * inv * jnp.mean(v * w, axis=1, keepdims=True))
    out[...] = grad
    low_out[...] = grad.astype(bf16)


def norm_back_call(x, du, got, dh, gain):
    rows, width = x.shape
    spec = pl.BlockSpec((rows // 2, width), lambda i: (i, 0))
    return pl.pallas_call(
        norm_back_kernel,
        grid=(2,),
        in_specs=[spec, spec, spec, spec, pl.BlockSpec((1, width), lambda i: (0, 0))],
        out_specs=[spec, spec],
        out_shape=[
            jax.ShapeDtypeStruct((rows, width), f32),
            jax.ShapeDtypeStruct((rows, width), bf16),
        ],
        compiler_params=params(10),
        cost_estimate=cost(1e7, 1e6),
        name="norm_back",
    )(x, du, got, dh, gain)


def home_kernel(stays, own, low, high, out):
    back = jnp.where(pl.program_id(0) == 0, low[...], high[...]).astype(f32)
    v = jnp.where(stays[0] == 1, own[...], back)
    n = v.shape[1] // 128
    for t in range(n):
        out[pl.ds(t, v.shape[0], stride=n), :] = v[:, t * 128 : (t + 1) * 128]


def home_call(stays, own, low, high):
    rows, width = own.shape
    n = width // 128
    spec = pl.BlockSpec((rows // 2, width), lambda i, s: (i, 0))
    out = pl.pallas_call(
        home_kernel,
        grid_spec=pltpu.PrefetchScalarGridSpec(
            num_scalar_prefetch=1,
            grid=(2,),
            in_specs=[spec, whole(low.shape), whole(high.shape)],
            out_specs=pl.BlockSpec((rows // 2 * n, 128), lambda i, s: (i, 0)),
        ),
        out_shape=jax.ShapeDtypeStruct((rows * n, 128), f32),
        compiler_params=params(8),
        cost_estimate=cost(1e7, 1e6),
        name="home",
    )(stays, own, low, high)
    return out.reshape(rows, 1, width)


def place_kernel(pieces, half, n_seq, per_shard, sc, own_core, twin, *rest):
    outs, box, sem = rest[:-2], rest[-2], rest[-1]
    core, place, own = sc[0], sc[2], sc[3]
    step = pl.program_id(0)
    parts, _, group = own_core.shape[:3]
    count = outs[0].shape[0]

    @pl.when(step == 0)
    def _():
        copies = []
        for c, source in enumerate((own_core, twin)):
            for part in range(parts):
                for k in range(half):
                    copies.append(
                        pltpu.make_async_copy(
                            source.at[part, k],
                            box.at[pl.ds(part * group, group), core ^ c, place ^ k],
                            sem.at[(c * parts + part) * half + k],
                        )
                    )
        for copy in copies:
            copy.start()
        for copy in copies:
            copy.wait()

    for out in outs:
        out[...] = jnp.zeros_like(out)
    for b in range(2 * n_seq):
        rel = own ^ b
        slot = sc[4 + b] - step * count

        @pl.when((slot >= 0) & (slot < count))
        def _():
            held = box.at[rel]
            into = [out.at[slot] for out in outs]
            for c in range(2):
                for index, target, lead, lane, shift in pieces:
                    at = lane + c * shift
                    rows = slice((index % per_shard) * R, (index % per_shard + 1) * R)
                    value = held[c, index // per_shard, rows, :].astype(f32)
                    into[target][lead + (slice(at, at + 128),)] += value


def place_call(steps, pieces, shapes, n_seq, sc, own_core, twin):
    parts, half, _, rows, _ = own_core.shape

    def out_spec(shape):
        zeros = (0,) * len(shape)
        return pl.BlockSpec((ADAPTER_SETS // steps,) + shape, lambda i, s: (i,) + zeros)

    return pl.pallas_call(
        functools.partial(place_kernel, pieces, half, n_seq, rows // R),
        grid_spec=pltpu.PrefetchScalarGridSpec(
            num_scalar_prefetch=1,
            grid=(steps,),
            in_specs=[pl.BlockSpec(memory_space=pl.ANY)] * 2,
            out_specs=[out_spec(shape) for shape in shapes],
            scratch_shapes=[
                pltpu.VMEM((2 * n_seq, 2, half, rows, 128), bf16),
                pltpu.SemaphoreType.DMA((2 * parts * half,)),
            ],
        ),
        out_shape=[jax.ShapeDtypeStruct((ADAPTER_SETS,) + shape, f32) for shape in shapes],
        compiler_params=params(24),
        cost_estimate=cost(1e7, 1e6),
        name="place",
    )(sc, own_core, twin)


def rope_parts():
    freq = np.exp(-math.log(rope_base) * 2.0 * np.arange(HEAD_SIZE // 2) / HEAD_SIZE)
    angle = np.arange(CH)[:, None] * freq[None, :]
    return freq, np.cos(angle).astype(np.float32), np.sin(angle).astype(np.float32)


def rope_tables(stretches):
    freq, cos_t, sin_t = rope_parts()
    angle = (stretches.astype(f32) * CH)[:, None] * jnp.asarray(freq.astype(np.float32))[None, :]
    cos_a, sin_a = jnp.cos(angle)[:, None, :], jnp.sin(angle)[:, None, :]
    cos = cos_a * cos_t[None] - sin_a * sin_t[None]
    sin = sin_a * cos_t[None] + cos_a * sin_t[None]
    return (
        jnp.concatenate([cos, cos, cos, cos], axis=-1).reshape(TOK, PAIR),
        jnp.concatenate([-sin, sin, -sin, sin], axis=-1).reshape(TOK, PAIR),
    )


def after(value, *earlier):
    return lax.optimization_barrier((value,) + earlier)[0]


def per_device(
    hidden_in, cotangent, query_key_value_weight, w_o, w_gu, w_down, g_attn, g_ffn, g_q,
    key_norm_gain, a_qkv, b_q, key_up_weight, value_up_weight, a_o, b_o, a_gu, b_gu, a_down,
    b_down, set_index, stretch_order,
):
    rows, _, width = hidden_in.shape
    n_ctx = lax.axis_size("ctx")
    n_seq = lax.axis_size("seq")
    half = n_ctx // 2
    core = lax.axis_index("wsh")
    ctx = lax.axis_index("ctx")
    side = ctx // half
    place = ctx % half
    own_seq = lax.axis_index("seq") * 2 + side
    stays = core == side

    def line(s, p, c):
        return (s * half + p) * 2 + c

    swap_pairs = [
        (line(s, p, c), line(c, p, s))
        for s in range(2) for p in range(half) for c in range(2) if s != c
    ]

    def swap(v):
        return lax.ppermute(v, ("ctx", "wsh"), swap_pairs)

    def other_core(v):
        return lax.ppermute(v, "wsh", [(0, 1), (1, 0)])

    def partner(v, k):
        return lax.ppermute(
            v, "ctx", [(s * half + p, s * half + (p ^ k)) for s in range(2) for p in range(half)]
        )

    def other_seq(v, d):
        pairs = [
            (s * n_ctx + i, (s ^ (d // 2)) * n_ctx + (i + half * (d % 2)) % n_ctx)
            for s in range(n_seq) for i in range(n_ctx)
        ]
        return lax.ppermute(v, ("seq", "ctx"), pairs)

    hid = hidden_in.reshape(rows, width)
    cot = cotangent.reshape(rows, width)
    mine = jnp.where(stays, hid, swap(hid))
    order = jnp.where(stays, stretch_order[0], swap(stretch_order)[0])
    other = other_core(mine)

    query_key_value_weight = after(query_key_value_weight, order)

    def cols(w, start, size, which):
        return lax.dynamic_slice_in_dim(w, start + which * size, size, 1)

    def qkv_cols(which):
        return jnp.concatenate(
            [
                cols(query_key_value_weight, 0, QW, which),
                cols(query_key_value_weight, 2 * QW, KW, which),
                cols(query_key_value_weight, 2 * QW + 2 * KW, KW, which),
            ],
            axis=1,
        )

    w_own = qkv_cols(core)
    w_send = after(qkv_cols(1 - core), mine)
    w_rec_q, w_rec_kv = other_core(w_send[:, :QW]), other_core(w_send[:, QW:])

    own_set = lax.dynamic_index_in_dim(set_index, own_seq, keepdims=False)
    low = order.reshape(2, half, 2)
    here = lax.dynamic_index_in_dim(low, place, 1, keepdims=False)
    flags = []
    for k in range(half):
        there = lax.dynamic_index_in_dim(low, place ^ k, 1, keepdims=False)
        flags.append((there[None, :, 0] < here[:, None, 0]).astype(jnp.int32).reshape(4))
    sc = jnp.concatenate(
        [jnp.stack([core, own_set, place, own_seq]).astype(jnp.int32), set_index] + flags
    )
    base = flag_base(n_seq)
    cos, sin = rope_tables(here.T.reshape(4))
    ones = jnp.asarray(np.kron(np.eye(4), np.ones((HEAD_SIZE, HEAD_SIZE))), bf16)
    gain_a = g_attn.astype(f32)[None]
    gain_f = g_ffn.astype(f32)[None]
    g_qk = jnp.concatenate(
        [jnp.tile(g_q, QW // HEAD_SIZE), jnp.tile(key_norm_gain, KW // HEAD_SIZE)]
    ).astype(f32)[None]
    a_qkv_t = jnp.swapaxes(a_qkv, 1, 2)
    a_o_t = jnp.swapaxes(a_o, 1, 2)
    a_gu_t = jnp.swapaxes(a_gu, 1, 2)
    a_down_t = jnp.swapaxes(a_down, 1, 2)

    u, raw, qm, kv = qkv_call(
        sc, mine, other, cos, sin, w_own, w_rec_q, w_rec_kv, gain_a, a_qkv_t, b_q, key_up_weight,
        value_up_weight, g_qk, ones,
    )
    kvs = [kv] + [partner(kv, k) for k in range(1, half)]
    acc = attend_call([base], sc, qm, [kv], None)
    cot = after(cot, mine)
    c_mine = jnp.where(stays, cot, swap(cot))
    c_sent = after(c_mine, acc)
    d_hid, ed, drdT = hidden_back_call(
        sc, c_mine, other_core(c_sent[:CH]), other_core(c_sent[CH:]), w_down, a_down_t, b_down
    )
    w_gu_late = after(w_gu, kv)
    gu_send = jnp.concatenate(
        [cols(w_gu_late, 0, HF, 1 - core), cols(w_gu_late, FF, HF, 1 - core)], axis=1
    )
    gu_rec = other_core(after(gu_send, d_hid, *kvs))
    acc = attend_call(
        [base + 4 * k for k in range(1, half)], sc, qm, kvs[1:], after(acc, d_hid, gu_send)
    )
    ob, mix, lse = project_call(sc, acc, w_o, a_o_t, b_o)
    mix_got = other_core(mix)
    y, down, du, pay_early = ffn_call(
        half, sc, mine, other, mix, mix_got, d_hid, ed, drdT, gain_f, w_gu, gu_rec, w_down,
        a_gu_t, b_gu, a_down_t, b_down,
    )
    dh, dom, delta, pay_early = back_mix_call(
        half, sc, mine, other, mix, mix_got, ed, du, other_core(du), gain_f, w_o, a_o_t, b_o, ob,
        ones, pay_early,
    )

    def summed(pay):
        shards = pay.reshape(half, -1, 128)
        total = shards[0].astype(f32)
        for k in range(1, half):
            total += partner(shards[k], k).astype(f32)
        return total.astype(bf16)

    layer = y + other_core(down).astype(f32)
    layer_low = swap(layer.astype(bf16))
    dq = None
    got = []
    early = summed(pay_early)
    for k in list(range(1, half)) + [0]:
        dq, dkv = attend_back_call(base + 4 * k, k == 0, sc, qm, dom, kvs[k], lse, delta, dq)
        if k:
            got.append(partner(dkv, k))
        if k == half - 2:
            dq = after(dq, early, layer_low)
    early = jnp.stack([early, other_seq(early, 1)])
    early = after(early, dq, *got)
    early_got = [early] + [partner(early, k) for k in range(1, half)]

    du_own, du_send, pay_late = qkv_back_call(
        half, sc, dq, dkv, got, raw, cos, sin, g_qk, ones, u, w_own, w_rec_q, w_rec_kv, a_qkv_t, b_q,
        key_up_weight, value_up_weight,
    )
    early = jnp.stack([after(v, pay_late) for v in early_got])
    early_got = [early] + [other_seq(early, 2 * d) for d in range(1, n_seq)]
    grad_in, grad_low = norm_back_call(mine, du_own, other_core(du_send), dh, gain_a)
    late = after(summed(pay_late), grad_low)
    late = jnp.stack([late] + [other_seq(late, d) for d in range(1, 2 * n_seq)])
    early = jnp.stack([after(v, late) for v in early_got])
    early_twin = other_core(early)
    back = swap(grad_low)
    back_low, back_high = back[:CH], back[CH:]

    stay_flag = stays.astype(jnp.int32).reshape(1)
    layer_out = home_call(stay_flag, layer, layer_low[:CH], layer_low[CH:])
    input_grad = home_call(stay_flag, grad_in, back_low, back_high)


    n_w = width // 128
    pieces = []
    for t in range(HF // 128):
        for q in range(2):
            pieces.append((t * 3 + q, 0, (q, slice(0, R)), t * 128, HF))
        pieces.append((t * 3 + 2, 1, (slice(0, R),), t * 128, HF))
    for t in range(n_w):
        pieces.append((GU_TILES + t, 2, (slice(0, R),), t * 128, 0))
        for q in range(2):
            rows_at = (slice(q * R, (q + 1) * R),)
            pieces.append((GU_TILES + n_w + t * 2 + q, 3, rows_at, t * 128, 0))
    for t in range(n_w):
        pieces.append((GU_TILES + 3 * n_w + t, 4, (slice(0, R),), t * 128, 0))
    for t in range(QW // 128):
        pieces.append((GU_TILES + 4 * n_w + t, 5, (slice(0, R),), t * 128, QW))
    r_gu, r_ad, r_bd, r_agu, r_bo, r_ao = place_call(
        2, pieces,
        [(2, R, FF), (R, FF), (R, width), (2 * R, width), (R, width), (R, 2 * QW)],
        n_seq, sc, early, early_twin,
    )

    late = [late] + [partner(late, k) for k in range(1, half)]
    late = jnp.stack([after(v, r_gu) for v in late])[None]
    late_twin = after(other_core(late), input_grad)

    pieces = []
    first_rows = (slice(0, R),)
    for t in range(n_w):
        for q in range(3):
            pieces.append((t * 3 + q, 0, (slice(q * R, (q + 1) * R),), t * 128, 0))
    for t in range(EW // 128):
        at = 3 * n_w + t
        if t < QW // 128:
            pieces.append((at, 1, first_rows, t * 128, QW))
        elif t < (QW + KW) // 128:
            pieces.append((at, 2, first_rows, t * 128 - QW, KW))
        else:
            pieces.append((at, 3, first_rows, t * 128 - QW - KW, KW))
    r_aqkv, r_bq, r_bk, r_bv = place_call(
        1, pieces,
        [(3 * R, width), (R, 2 * QW), (R, 2 * KW), (R, 2 * KW)],
        n_seq, sc, late, late_twin,
    )
    return (
        layer_out,
        input_grad,
        jnp.swapaxes(r_aqkv, 1, 2),
        r_bq,
        r_bk,
        r_bv,
        jnp.swapaxes(r_ao, 1, 2),
        r_bo,
        jnp.swapaxes(r_agu, 1, 2),
        r_gu,
        jnp.swapaxes(r_ad, 1, 2),
        r_bd,
    )


def solution(mesh):
    tokens = P("ctx", ("seq", "wsh"), None)
    in_specs = (
        (tokens, tokens) + (P("wsh", None),) * 4 + (P(),) * 15 + (P(("seq", "wsh"), None),)
    )
    out_specs = (tokens, tokens) + (P(),) * 10
    return jax.shard_map(
        per_device, mesh=mesh, in_specs=in_specs, out_specs=out_specs, check_vma=False
    )
```
